128 devices in a mesh: pos: 16 (over y, x_hi, core), off: 8 (over z, x_lo).
Axes of the slice: x: 4 (x_hi: 2, x_lo: 2; x = x_hi * 2 + x_lo), y: 4, z: 4, core: 2. Of those that a mesh axis runs over, the one named last changes fastest.
Arguments:
- band_map: bfloat16 [48, 2304, 2048], P(None, 'pos', 'off'), may hold values from -6 to 6
- dilations: int32 [2], replicated, may hold values from 1 to 32, as said below
- row_limit: int32 [2304], replicated, may hold values from 512 to 1023
- weight_one: bfloat16 [9, 48, 48], replicated, may hold values from -0.3125 to 0.3125
- bias_one: float32 [48], replicated, may hold values from -3 to 3
- weight_two: bfloat16 [9, 48, 48], replicated, may hold values from -0.3125 to 0.3125
- bias_two: float32 [48], replicated, may hold values from -3 to 3
Outputs:
- mixed: bfloat16 [48, 2304, 2048], P(None, 'pos', 'off')
The draws below stay inside these ranges and needn't reach their ends.
Inputs may be any that keep to these rules, and one draw needn't show every extreme that they name: One of the two dilations equals 32.
All inputs are finite; a program needn't handle non-finite values.
Results may differ from the reference program's by a relative error of at most 0.0052.
Values may be sent and summed in bfloat16 or wider, within the bound.
No kernel may reach another device: no remote copies, remote signals or barrier semaphores. Data moves between devices by JAX's collectives and lax.ppermute only.
A program may use at most 384 MiB of HBM per device.

```python
import jax
import jax.numpy as jnp
from jax import lax

C = 48
BAND = 1024
DMAX = 32
ROWS_DEV = 144
NPOS = 2304
NOFF = 2048


def draw_dilations(key, part):
    key = jax.random.fold_in(key, 11)
    key_one, key_two = jax.random.split(key)
    other_rates = jax.random.randint(key_one, (2,), 1, DMAX + 1)
    which_one = jax.random.randint(key_two, (), 0, 2)
    positions = jnp.arange(2)
    return jnp.where(positions == which_one, DMAX, other_rates).astype(jnp.int32)


def draw_row_limit(key, part):
    key = jax.random.fold_in(key, 23)
    key_one, key_two, key_three = jax.random.split(key, 3)
    limits = jax.random.randint(key_one, (NPOS,), BAND // 2, BAND)
    top_place = jax.random.randint(key_two, (), 0, NPOS)
    low_place = jax.random.randint(key_three, (), 0, NPOS)
    positions = jnp.arange(NPOS)
    limits = jnp.where(positions == top_place, BAND - 1, limits)
    limits = jnp.where((positions == low_place) & (positions != top_place), BAND // 2, limits)
    return limits.astype(jnp.int32)


def levels(stream_key, dims, pieces, smallest, high):
    factor_of = 1.0
    for axis_at, shards_of in pieces:
        heights = jax.random.uniform(jax.random.fold_in(jax.random.fold_in(stream_key, 6), axis_at), (shards_of,), jnp.float32, smallest / len(pieces), high / len(pieces))
        factor_of = factor_of * jnp.repeat(jnp.exp(heights), dims[axis_at] // shards_of).reshape((-1,) + (1,) * (len(dims) - 1 - axis_at))
    return factor_of


def bell_draw(key, extent, spread, most, pieces=(), held_as=jnp.bfloat16):
    drawn = spread * jax.random.normal(key, extent, jnp.float32)
    if pieces:
        drawn = drawn * levels(key, extent, pieces, -0.22, 0.18)
    return jnp.clip(drawn, -most, most).astype(held_as)


def setup_inputs(seed: int = 0) -> dict:
    key_of = jax.random.split(jax.random.key(seed), 8)
    return {
        "band_map": bell_draw(key_of[0], (C, NPOS, NOFF), 1.0, 6.0, ((1, 16), (2, 8))),
        "dilations": draw_dilations(jax.random.fold_in(key_of[7], 71), 0),
        "row_limit": draw_row_limit(jax.random.fold_in(key_of[7], 71), 0),
        "weight_one": bell_draw(key_of[3], (9, C, C), (9 * C) ** -0.5, 0.3125),
        "bias_one": bell_draw(key_of[4], (C,), 0.5, 3.0, (), jnp.float32),
        "weight_two": bell_draw(key_of[5], (9, C, C), (9 * C) ** -0.5, 0.3125),
        "bias_two": bell_draw(key_of[6], (C,), 0.5, 3.0, (), jnp.float32),
    }


def valid_mask(row_ids, col_ids, limits, total_rows):
    offset_cols = col_ids - BAND
    parity_cols = col_ids % 2
    first_bin = row_ids[:, None] + ((parity_cols - offset_cols) // 2)[None, :]
    second_bin = row_ids[:, None] + ((parity_cols + offset_cols) // 2)[None, :]
    inside = (first_bin >= 0) & (first_bin < total_rows) & (second_bin >= 0) & (second_bin < total_rows)
    return inside & (jnp.abs(offset_cols)[None, :] <= limits[:, None])


def dilated_conv(padded, weight, dilation, row_count, col_count, margin):
    channels = padded.shape[0]
    odd_cols = (jnp.arange(col_count) % 2 == 1)[None, None, :]
    accum_sum = jnp.zeros((weight.shape[1], row_count, col_count), jnp.float32)
    tap_index = 0
    for row_sign in (-1, 0, 1):
        for col_sign in (-1, 0, 1):
            row_step = dilation * (row_sign + col_sign)
            col_step = dilation * (col_sign - row_sign)
            col_first = (margin + col_step).astype(jnp.int32)
            low_start = (margin + row_step // 2).astype(jnp.int32)
            high_start = (margin + (row_step + 1) // 2).astype(jnp.int32)
            low_slice = lax.dynamic_slice(padded, (jnp.int32(0), low_start, col_first), (channels, row_count, col_count))
            high_slice = lax.dynamic_slice(padded, (jnp.int32(0), high_start, col_first), (channels, row_count, col_count))
            picked = jnp.where(odd_cols, high_slice, low_slice)
            accum_sum = accum_sum + jnp.einsum("oc,crk->ork", weight[tap_index].astype(jnp.float32), picked.astype(jnp.float32), precision=lax.Precision.HIGHEST)
            tap_index += 1
    return accum_sum


def reference(band_map, dilations, row_limit, weight_one, bias_one, weight_two, bias_two):
    margin = 2 * DMAX
    all_rows = jnp.arange(NPOS, dtype=jnp.int32)
    all_cols = jnp.arange(NOFF, dtype=jnp.int32)
    valid_full = valid_mask(all_rows, all_cols, row_limit, NPOS)
    masked = jnp.where(valid_full[None], band_map, jnp.zeros((), jnp.bfloat16))
    padded = jnp.pad(masked, ((0, 0), (2 * margin, 2 * margin), (2 * margin, 2 * margin)))
    block_count = NPOS // ROWS_DEV

    def one_block(block_index):
        start = (block_index * ROWS_DEV).astype(jnp.int32)
        window = lax.dynamic_slice(padded, (jnp.int32(0), start, jnp.int32(0)), (C, ROWS_DEV + 4 * margin, NOFF + 4 * margin))
        wide_rows = start - margin + jnp.arange(ROWS_DEV + 2 * margin, dtype=jnp.int32)
        wide_cols = jnp.arange(NOFF + 2 * margin, dtype=jnp.int32) - margin
        wide_limits = jnp.take(row_limit, jnp.clip(wide_rows, 0, NPOS - 1))
        wide_valid = valid_mask(wide_rows, wide_cols, wide_limits, NPOS)
        first = dilated_conv(window, weight_one, dilations[0], ROWS_DEV + 2 * margin, NOFF + 2 * margin, margin) + bias_one[:, None, None]
        hidden = jnp.where(wide_valid[None], jnp.maximum(first, 0.0), 0.0).astype(jnp.bfloat16)
        second = dilated_conv(hidden, weight_two, dilations[1], ROWS_DEV, NOFF, margin) + bias_two[:, None, None]
        own_part = lax.dynamic_slice_in_dim(masked, start, ROWS_DEV, 1).astype(jnp.float32)
        own_valid = lax.dynamic_slice_in_dim(valid_full, start, ROWS_DEV, 0)
        return jnp.where(own_valid[None], second + own_part, 0.0).astype(jnp.bfloat16)

    blocks = lax.map(one_block, jnp.arange(block_count, dtype=jnp.int32))
    summed = jnp.transpose(blocks, (1, 0, 2, 3)).reshape(C, NPOS, NOFF)
    mirrored = jnp.concatenate([jnp.zeros((C, NPOS, 1), jnp.bfloat16), summed[:, :, :0:-1]], axis=2)
    mixed = jnp.where(valid_full[None], 0.5 * (summed.astype(jnp.float32) + mirrored.astype(jnp.float32)), 0.0)
    return mixed.astype(jnp.bfloat16)
```

```python
import functools

import jax
import jax.numpy as jnp
from jax import lax
from jax.experimental import pallas as pl
from jax.experimental.pallas import tpu as pltpu
from jax.sharding import PartitionSpec as P

BAND = 1024
DMAX = 32
C = 48
ROWS = 144
COLS = 256
LANES = 128
HALO = DMAX
PAIR = ROWS // 2
CORNER = DMAX // 2
GROUP = CORNER // 4
CHUNK = 48
PARTS = ROWS // CHUNK
PREP = 8
AXES = ("pos", "off")

SMEM = pl.BlockSpec(memory_space=pltpu.SMEM)
VMEM = pl.BlockSpec(memory_space=pltpu.VMEM)
ANY = pl.BlockSpec(memory_space=pl.ANY)
PARAMS = pltpu.CompilerParams(vmem_limit_bytes=56 * 2**20)

PLANE_OF_FOLD = (0, 3, 2, 1)
FOLD_OF_PLANE = (0, 3, 2, 1)


def home(strip, block):
    return strip * 8 + block


def place(strip, block):
    fold = min(block, 7 - block)
    core = 1 if block >= 4 else 0
    return (2 * (strip // 2) + core) * 8 + 2 * PLANE_OF_FOLD[fold] + strip % 2


def grid_cells():
    return [(strip, block) for strip in range(16) for block in range(8)]


def moves(strip_step, block_step):
    return [
        (place(s, b), place(s + strip_step, b + block_step))
        for s, b in grid_cells()
        if 0 <= s + strip_step < 16 and 0 <= b + block_step < 8
    ]


def worked_cell():
    pos, off = lax.axis_index("pos"), lax.axis_index("off")
    strip = 2 * (pos // 2) + off % 2
    fold = jnp.array(FOLD_OF_PLANE, jnp.int32)[off // 2]
    return strip, jnp.where(pos % 2 == 1, 7 - fold, fold)


def thresholds(row_limit, strip):
    rows = strip * ROWS + jnp.arange(ROWS, dtype=jnp.int32)
    limit = lax.dynamic_slice(row_limit, (strip * ROWS,), (ROWS,))
    last = row_limit.shape[0] - 1
    return jnp.minimum(limit, jnp.minimum(2 * rows + 1, 2 * last - 2 * rows))


def offsets(col, shape):
    return jnp.abs(lax.broadcasted_iota(jnp.int32, shape, len(shape) - 1) + col)


def spans(first, count, cuts):
    out = []
    at = first
    while at < first + count:
        end = min([c for c in cuts if c > at] + [first + count])
        out.append((at, end - at))
        at = end
    return out


def enter_kernel(part, t_ref, col_ref, x_ref, out_ref):
    x = jnp.swapaxes(x_ref[...], 0, 1)
    for i in range(CHUNK):
        seen = offsets(col_ref[0], (C, COLS)) <= t_ref[part * CHUNK + i]
        out_ref[i] = jnp.where(seen, x[i], jnp.zeros((), jnp.bfloat16))


def enter(part, limits, col, band_map):
    return pl.pallas_call(
        functools.partial(enter_kernel, part),
        grid=(1,),
        in_specs=[SMEM, SMEM, pl.BlockSpec((C, CHUNK, COLS), lambda i: (0, part, 0))],
        out_specs=pl.BlockSpec((CHUNK, C, COLS), lambda i: (0, 0, 0)),
        out_shape=jax.ShapeDtypeStruct((CHUNK, C, COLS), jnp.bfloat16),
        compiler_params=PARAMS,
        name="enter",
    )(limits, col, band_map)


def pack_edges(load, top, bottom, left, right, corners):
    lane = lax.broadcasted_iota(jnp.int32, (C, LANES), 1)
    for i in range(PAIR):
        a, b = load(i), load(i + PAIR)
        left[i] = jnp.where(lane < 64, a[:, :LANES], pltpu.roll(b[:, :LANES], 64, axis=1))
        right[i] = jnp.where(lane < 64, pltpu.roll(a[:, LANES:], 64, axis=1), b[:, LANES:])
    for i in range(HALO):
        top[i] = load(i)
        bottom[i] = load(ROWS - HALO + i)
    for ref, first, side in zip(corners, (0, 0, ROWS - CORNER, ROWS - CORNER), (0, 1, 0, 1)):
        for i in range(GROUP):
            packed = None
            for g in range(4):
                cells = load(first + g * GROUP + i)
                cells = cells[:, LANES:] if side else cells[:, :LANES]
                turn = (32 * g + (32 if side else 0)) % LANES
                cells = pltpu.roll(cells, turn, axis=1) if turn else cells
                packed = cells if packed is None else jnp.where(lane < 32 * g, packed, cells)
            ref[i] = packed


EDGES = (
    [jax.ShapeDtypeStruct((HALO, C, COLS), jnp.bfloat16)] * 2
    + [jax.ShapeDtypeStruct((PAIR, C, LANES), jnp.bfloat16)] * 2
    + [jax.ShapeDtypeStruct((GROUP, C, LANES), jnp.bfloat16)] * 4
)


def pack_kernel(*refs):
    parts, edges = refs[:PARTS], refs[PARTS:]

    def load(row):
        return parts[row // CHUNK][row % CHUNK]

    pack_edges(load, *edges[:4], edges[4:])


def pack(parts):
    return pl.pallas_call(
        pack_kernel,
        in_specs=[VMEM] * PARTS,
        out_specs=[VMEM] * 8,
        out_shape=EDGES,
        compiler_params=PARAMS,
        name="pack",
    )(*parts)


def exchange(edges):
    top, bottom, left, right, up_left, up_right, down_left, down_right = edges
    send = lambda cells, step: lax.ppermute(cells, AXES, moves(*step))
    from_right = send(left, (0, -1))
    from_left = send(right, (0, 1))
    from_below = send(top, (-1, 0))
    from_above = send(bottom, (1, 0))
    corners = (
        send(down_right, (1, 1)),
        send(down_left, (1, -1)),
        send(up_right, (-1, 1)),
        send(up_left, (-1, -1)),
    )
    return from_above, from_below, from_left, from_right, corners


def conv_kernel(first, count, final, *refs):
    d_ref, col_ref, t_ref = refs[:3]
    parts = refs[3 : 3 + PARTS]
    above, below, from_left, from_right = refs[3 + PARTS : 7 + PARTS]
    corners = refs[7 + PARTS : 11 + PARTS]
    w_ref, b_ref = refs[11 + PARTS : 13 + PARTS]
    rest = refs[13 + PARTS :]
    if final:
        own_ref, out_ref, edge_ref, mid, lft, rgt, plus_ref, minus_ref, sems = rest
    else:
        out_ref, *edges = rest[:9]
        mid, lft, rgt, plus_ref, minus_ref, sems = rest[9:]

    base = first - HALO
    copies = []
    for at, size in spans(base, count + 2 * HALO, [0] + [CHUNK * i for i in range(1, PARTS + 1)]):
        if at < 0:
            src = above.at[pl.ds(at + HALO, size)]
        elif at >= ROWS:
            src = below.at[pl.ds(at - ROWS, size)]
        else:
            src = parts[at // CHUNK].at[pl.ds(at % CHUNK, size)]
        copies.append(pltpu.make_async_copy(src, mid.at[pl.ds(at - base, size)], sems.at[len(copies)]))
    for copy in copies:
        copy.start()

    for at, size in spans(first - CORNER, count + 2 * CORNER, [0, PAIR, ROWS]):
        for j in range(size):
            row = at + j
            if row < 0 or row >= ROWS:
                i = row + CORNER if row < 0 else row - ROWS
                pair = corners[:2] if row < 0 else corners[2:]
                g, i = i // GROUP, i % GROUP
                a, b = pair[0][i], pair[1][i]
                lft[row - base] = pltpu.roll(a, 96 - 32 * g, axis=1) if g != 3 else a
                rgt[row - base] = pltpu.roll(b, 128 - 32 * g, axis=1) if g else b
            elif row < PAIR:
                lft[row - base] = pltpu.roll(from_left[row], 64, axis=1)
                rgt[row - base] = from_right[row]
            else:
                lft[row - base] = from_left[row - PAIR]
                rgt[row - base] = pltpu.roll(from_right[row - PAIR], 64, axis=1)
    for copy in copies:
        copy.wait()

    d = d_ref[0]
    lo = d // 2
    hi = (d + 1) // 2
    odd = d - 2 * lo
    lane = lax.broadcasted_iota(jnp.int32, (C, LANES), 1)
    even_lane = (lane & 1) == 0

    def tiles(r):
        return [lft[r], mid[r, :, :LANES], mid[r, :, LANES:], rgt[r]]

    def onward(t, step):
        keep = lane < LANES - step
        a, b, c = [pltpu.roll(x, LANES - step, axis=1) for x in t[1:]]
        return jnp.concatenate([jnp.where(keep, a, b), jnp.where(keep, b, c)], axis=1)

    def backward(t, step):
        keep = lane < step
        a, b, c = [pltpu.roll(x, step, axis=1) for x in t[:3]]
        return jnp.concatenate([jnp.where(keep, a, b), jnp.where(keep, b, c)], axis=1)

    start = HALO - hi

    def prepare(i, _):
        for j in range(PREP):
            r = start + i * PREP + j
            x, y = tiles(r), tiles(r + odd)
            cells = [jnp.where(even_lane, b, a) for a, b in zip(x, y)]
            plus_ref[r] = onward(cells, d)
            minus_ref[r] = backward(cells, d)
        return 0

    lax.fori_loop(0, (count + d + PREP - 1) // PREP, prepare, 0)

    weight = w_ref[...]
    bias = b_ref[...]
    col = col_ref[0]
    if final:
        edge_ref[...] = jnp.zeros_like(edge_ref)

    def row(m, _):
        r = m + HALO
        x = tiles(r)
        taps = [
            mid[r - d],
            plus_ref[r - hi],
            onward(x, 2 * d),
            minus_ref[r - hi],
            mid[r],
            plus_ref[r + lo],
            backward(x, 2 * d),
            minus_ref[r + lo],
            mid[r + d],
        ]
        acc = lax.dot_general(
            weight,
            jnp.concatenate(taps, axis=0),
            (((1,), (0,)), ((), ())),
            preferred_element_type=jnp.float32,
        )
        acc = acc + bias
        if final:
            acc = acc + own_ref[m].astype(jnp.float32)
        else:
            acc = jnp.maximum(acc, 0.0)
        acc = jnp.where(offsets(col, (C, COLS)) <= t_ref[first + m], acc, 0.0).astype(jnp.bfloat16)
        out_ref[m] = acc
        if final:
            edge_ref[...] = jnp.where(lane == m, pltpu.roll(acc[:, :LANES], m, axis=1), edge_ref[...])
        return 0

    lax.fori_loop(0, count, row, 0, unroll=8)
    if not final:
        pack_edges(lambda i: out_ref[i], *edges[:4], edges[4:])


def conv(first, count, final, d, col, limits, parts, halos, weight, bias):
    above, below, from_left, from_right, corners = halos
    wide = count + 2 * HALO
    in_specs = [SMEM] * 3 + [ANY] * (PARTS + 2) + [VMEM] * 8
    args = [d, col, limits, *parts, above, below, from_left, from_right, *corners, weight, bias]
    if final:
        in_specs.append(VMEM)
        args.append(final[first // CHUNK])
    out_shape = [jax.ShapeDtypeStruct((count, C, COLS), jnp.bfloat16)]
    if final:
        out_shape.append(jax.ShapeDtypeStruct((C, LANES), jnp.bfloat16))
    else:
        out_shape += EDGES
    return pl.pallas_call(
        functools.partial(conv_kernel, first, count, bool(final)),
        in_specs=in_specs,
        out_specs=[VMEM] * len(out_shape),
        out_shape=out_shape,
        scratch_shapes=[
            pltpu.VMEM((wide, C, COLS), jnp.bfloat16),
            pltpu.VMEM((wide, C, LANES), jnp.bfloat16),
            pltpu.VMEM((wide, C, LANES), jnp.bfloat16),
            pltpu.VMEM((wide, C, COLS), jnp.bfloat16),
            pltpu.VMEM((wide, C, COLS), jnp.bfloat16),
            pltpu.SemaphoreType.DMA((PARTS + 2,)),
        ],
        compiler_params=PARAMS,
        cost_estimate=pl.CostEstimate(
            flops=2 * 9 * C * C * COLS * count * 10, bytes_accessed=wide * C * COLS * 8, transcendentals=0
        ),
        name="second" if final else "first",
    )(*args)


def mix_kernel(part, t_ref, col_ref, own_ref, twin_ref, edge_ref, out_ref, rows_ref):
    lane = lax.broadcasted_iota(jnp.int32, (C, LANES), 1)
    a = lax.broadcasted_iota(jnp.int32, (COLS, COLS), 0)
    b = lax.broadcasted_iota(jnp.int32, (COLS, COLS), 1)
    turn = ((a + b == COLS) | (a + b == 0)).astype(jnp.bfloat16)
    edge = edge_ref[...]
    for m in range(CHUNK):
        twin = twin_ref[m]
        head = pltpu.roll(edge, LANES - m, axis=1) if m else edge
        twin = jnp.concatenate([jnp.where(lane == 0, head, twin[:, :LANES]), twin[:, LANES:]], axis=1)
        mirror = jnp.dot(twin, turn, preferred_element_type=jnp.float32)
        both = 0.5 * (own_ref[m].astype(jnp.float32) + mirror)
        seen = offsets(col_ref[0], (C, COLS)) <= t_ref[part * CHUNK + m]
        rows_ref[m] = jnp.where(seen, both, 0.0).astype(jnp.bfloat16)
    out_ref[...] = jnp.swapaxes(rows_ref[...], 0, 1)


def mix(part, limits, col, own, twin, edge):
    return pl.pallas_call(
        functools.partial(mix_kernel, part),
        in_specs=[SMEM] * 2 + [VMEM] * 3,
        out_specs=VMEM,
        out_shape=jax.ShapeDtypeStruct((C, CHUNK, COLS), jnp.bfloat16),
        scratch_shapes=[pltpu.VMEM((CHUNK, C, COLS), jnp.bfloat16)],
        compiler_params=PARAMS,
        name="mix",
    )(limits, col, own, twin, edge)


def flat(weight):
    return jnp.transpose(weight, (1, 0, 2)).reshape(C, 9 * C)


def local(band_map, dilations, row_limit, weight_one, bias_one, weight_two, bias_two):
    stored_strip, stored_block = lax.axis_index("pos"), lax.axis_index("off")
    strip, block = worked_cell()
    stored_limits = thresholds(row_limit, stored_strip)
    stored_col = (stored_block * COLS - BAND).reshape(1)
    limits = thresholds(row_limit, strip)
    col = (block * COLS - BAND).reshape(1)
    there = [(home(s, b), place(s, b)) for s, b in grid_cells()]
    back = [(b, a) for a, b in there]
    mirrored = [(place(s, b), place(s, 7 - b)) for s, b in grid_cells()]
    beyond = [(place(s, b), place(s, 8 - b)) for s, b in grid_cells() if b >= 1]

    parts = [
        lax.ppermute(enter(i, stored_limits, stored_col, band_map), AXES, there) for i in range(PARTS)
    ]
    halos = exchange(pack(parts))
    hidden, *edges = conv(
        0, ROWS, None, dilations[:1], col, limits, parts, halos, flat(weight_one), bias_one[:, None]
    )
    halos = exchange(edges)
    hidden = [lax.slice_in_dim(hidden, i * CHUNK, (i + 1) * CHUNK) for i in range(PARTS)]
    weight = flat(weight_two)
    out = []
    for i in range(PARTS):
        summed, edge = conv(
            i * CHUNK, CHUNK, parts, dilations[1:], col, limits, hidden, halos, weight, bias_two[:, None]
        )
        twin = lax.ppermute(summed, AXES, mirrored)
        edge = lax.ppermute(edge, AXES, beyond)
        mixed = mix(i, limits, col, summed, twin, edge)
        out.append(lax.ppermute(mixed, AXES, back))
    return jnp.concatenate(out, axis=1)


def solution(mesh):
    in_specs = (P(None, "pos", "off"), P(), P(), P(), P(), P(), P())
    out_specs = P(None, "pos", "off")
    return jax.shard_map(local, mesh=mesh, in_specs=in_specs, out_specs=out_specs, check_vma=False)
```

```python
import functools

import jax
import jax.numpy as jnp
from jax import lax
from jax.experimental import pallas as pl
from jax.experimental.pallas import tpu as pltpu
from jax.sharding import PartitionSpec as P

BAND = 1024
DMAX = 32
C = 48
ROWS = 72
COLS = 256
WIDE = 2 * COLS
LANES = 128
HALO = DMAX
CORNER = DMAX // 2
SPAN = ROWS + 2 * HALO
PREP = 4
UNROLL = 4
STACK = 8
AXES = ("pos", "off")

SMEM = pl.BlockSpec(memory_space=pltpu.SMEM)
VMEM = pl.BlockSpec(memory_space=pltpu.VMEM)
ANY = pl.BlockSpec(memory_space=pl.ANY)
PARAMS = pltpu.CompilerParams(vmem_limit_bytes=56 * 2**20)


def device(pair, x, z, core):
    return (2 * pair + core) * 8 + 2 * z + x


def home(stored, block):
    return device(stored // 2, block % 2, block // 2, stored % 2)


def place(strip, fold):
    stored = strip // 2
    return device(stored // 2, stored % 2, (4 - fold) % 4, strip % 2)


def lead(stored, fold):
    return (fold == 1) & (stored % 2 == 0) | (fold == 3) & (stored % 2 == 1)


CELLS = [(strip, fold) for strip in range(32) for fold in range(4)]


def routes(turn):
    out = []
    for strip, fold in CELLS:
        core, stored = strip % 2, strip // 2
        first = (core == int(lead(stored, fold))) == (turn == 0)
        out.append((home(stored, fold if first else 7 - fold), place(strip, fold)))
    return out


VIA = {(0, 1): (0, 0, 0), (0, 7): (0, 3, 0), (1, 2): (1, 1, 1), (1, 4): (1, 2, 1)}
STAY = ((0, 0), (0, 6), (1, 3), (1, 5))


def moves(strip_step, fold_step):
    return [
        (place(s, f), place(s + strip_step, f + fold_step))
        for s, f in CELLS
        if 0 <= s + strip_step < 32 and 0 <= f + fold_step < 4
    ]


def whereabouts():
    pos, off = lax.axis_index("pos"), lax.axis_index("off")
    fold = jnp.minimum(off, 7 - off)
    early = jnp.where(off < 4, 0, 1) ^ lead(pos, fold).astype(jnp.int32)
    stored = 2 * (pos // 2) + off % 2
    core = pos % 2
    work = (4 - off // 2) % 4
    order = core ^ lead(stored, work).astype(jnp.int32)
    values = (pos * 2 * ROWS, off, early, stored * 2 * ROWS + core * ROWS, work, order, core)
    return [v.astype(jnp.int32) for v in values]


STORED_ROW, STORED_BLOCK, EARLY, ROW, FOLD, ORDER, CORE = range(7)


def threshold(limit_ref, row):
    last = limit_ref.shape[0] - 1
    return jnp.minimum(limit_ref[row], jnp.minimum(2 * row + 1, 2 * last - 2 * row))


def offsets(block, dims):
    return jnp.abs(lax.broadcasted_iota(jnp.int32, dims, len(dims) - 1) + (block * COLS - BAND))


def both_offsets(fold):
    return jnp.concatenate([offsets(fold, (C, COLS)), offsets(7 - fold, (C, COLS))], axis=1)


def cost(micros):
    return pl.CostEstimate(flops=0, bytes_accessed=int(micros * 3.69e6), transcendentals=0)


def shape(*dims):
    return jax.ShapeDtypeStruct(dims, jnp.bfloat16)


def enter_kernel(turn, at_ref, limit_ref, x_ref, *rest):
    out_ref = rest[-1]
    x = jnp.swapaxes(x_ref[...], 0, 1)
    away = offsets(at_ref[STORED_BLOCK], (C, COLS))
    row0 = at_ref[STORED_ROW] + (at_ref[EARLY] ^ turn) * ROWS
    for i in range(ROWS):
        seen = away <= threshold(limit_ref, row0 + i)
        out_ref[i] = jnp.where(seen, x[i], jnp.zeros((), jnp.bfloat16))


def enter(turn, at, row_limit, band_map, after):
    return pl.pallas_call(
        functools.partial(enter_kernel, turn),
        grid_spec=pltpu.PrefetchScalarGridSpec(
            num_scalar_prefetch=1,
            grid=(1,),
            in_specs=[SMEM, pl.BlockSpec((C, ROWS, COLS), lambda i, at_ref: (0, at_ref[EARLY] ^ turn, 0))]
            + [ANY] * len(after),
            out_specs=pl.BlockSpec((ROWS, C, COLS), lambda i, at_ref: (0, 0, 0)),
        ),
        out_shape=shape(ROWS, C, COLS),
        compiler_params=PARAMS,
        cost_estimate=cost(4.0),
        name="enter",
    )(at, row_limit, band_map, *after)


EDGES = [shape(ROWS, C, LANES)] * 2 + [shape(HALO, C, WIDE)] * 2


def pack_edges(cells, inward, outward, top, bottom):
    lane = lax.broadcasted_iota(jnp.int32, (C, LANES), 1)
    for i in range(ROWS):
        inward[i] = jnp.where(lane < 64, cells[i, :, 2 * LANES : 3 * LANES], cells[i, :, LANES : 2 * LANES])
        outward[i] = jnp.where(lane < 64, cells[i, :, :LANES], cells[i, :, 3 * LANES :])
    top[...] = cells[pl.ds(0, HALO)]
    bottom[...] = cells[pl.ds(ROWS - HALO, HALO)]


def pack_kernel(at_ref, early_ref, late_ref, out_ref, *edges):
    @pl.when(at_ref[ORDER] == 0)
    def _():
        out_ref[:, :, :COLS] = early_ref[...]
        out_ref[:, :, COLS:] = late_ref[...]

    @pl.when(at_ref[ORDER] != 0)
    def _():
        out_ref[:, :, :COLS] = late_ref[...]
        out_ref[:, :, COLS:] = early_ref[...]

    pack_edges(out_ref, *edges)


def pack(at, early, late):
    out = [shape(ROWS, C, WIDE)] + EDGES
    return pl.pallas_call(
        pack_kernel,
        in_specs=[SMEM, VMEM, VMEM],
        out_specs=[VMEM] * len(out),
        out_shape=out,
        compiler_params=PARAMS,
        cost_estimate=cost(4.0),
        name="pack",
    )(at, early, late)


def send(cells, strip_step, fold_step):
    return lax.ppermute(cells, AXES, moves(strip_step, fold_step))


def exchange(at, inward, outward, top, bottom):
    previous = send(inward, 0, 1)
    following = send(outward, 0, -1)
    below = send(top, -1, 0)
    above = send(bottom, 1, 0)
    following = jnp.where(at[FOLD] == 3, inward, following)
    ends = lambda first: jnp.concatenate(
        [lax.slice_in_dim(x, first, first + CORNER) for x in (previous, following)], axis=0
    )
    corner_below = send(ends(0), -1, 0)
    corner_above = send(ends(ROWS - CORNER), 1, 0)
    return previous, following, above, below, corner_above, corner_below


def conv_kernel(final, at_ref, d_ref, limit_ref, cells, *refs):
    previous, following, above, below, corner_above, corner_below, w_ref, b_ref = refs[:8]
    if final:
        own_ref, first_ref, second_ref, edge_ref, other_ref = refs[8:13]
        out_ref, rest = refs[13], refs[14:]
    else:
        out_ref, edges, rest = refs[8], refs[9:13], refs[13:]
    mid, before, behind, plus_ref, minus_ref, sems = rest

    copies = [
        (above, mid.at[pl.ds(0, HALO)]),
        (cells, mid.at[pl.ds(HALO, ROWS)]),
        (below, mid.at[pl.ds(HALO + ROWS, HALO)]),
        (previous, before.at[pl.ds(HALO, ROWS)]),
        (following, behind.at[pl.ds(HALO, ROWS)]),
        (corner_above.at[pl.ds(0, CORNER)], before.at[pl.ds(HALO - CORNER, CORNER)]),
        (corner_above.at[pl.ds(CORNER, CORNER)], behind.at[pl.ds(HALO - CORNER, CORNER)]),
        (corner_below.at[pl.ds(0, CORNER)], before.at[pl.ds(HALO + ROWS, CORNER)]),
        (corner_below.at[pl.ds(CORNER, CORNER)], behind.at[pl.ds(HALO + ROWS, CORNER)]),
    ]
    copies = [pltpu.make_async_copy(src, dst, sems.at[i]) for i, (src, dst) in enumerate(copies)]
    for copy in copies:
        copy.start()
    for copy in copies:
        copy.wait()

    d = d_ref[0]
    lo = d // 2
    hi = (d + 1) // 2
    odd = d - 2 * lo
    lane = lax.broadcasted_iota(jnp.int32, (C, LANES), 1)
    even_lane = (lane & 1) == 0

    def tiles(r):
        own = [mid[r, :, LANES * i : LANES * (i + 1)] for i in range(4)]
        return [before[r], *own[:2], behind[r], *own[2:]]

    def shifted(t, step, back):
        keep = lane < (step if back else LANES - step)
        turn = step if back else LANES - step
        left, a, b, right, c, e = t
        runs = ((left, a, b), (right, c, e)) if back else ((a, b, right), (c, e, left))
        out = []
        for run in runs:
            x, y, z = [pltpu.roll(v, turn, axis=1) for v in run]
            out += [jnp.where(keep, x, y), jnp.where(keep, y, z)]
        return jnp.concatenate(out, axis=1)

    start = HALO - hi

    def prepare(i, _):
        for j in range(PREP):
            r = start + i * PREP + j
            x, y = tiles(r), tiles(r + odd)
            both = [jnp.where(even_lane, b, a) for a, b in zip(x, y)]
            plus_ref[r] = shifted(both, d, False)
            minus_ref[r] = shifted(both, d, True)
        return 0

    lax.fori_loop(0, (ROWS + d + PREP - 1) // PREP, prepare, 0)

    weight = w_ref[...]
    bias = b_ref[...]
    away = both_offsets(at_ref[FOLD])
    row0 = at_ref[ROW]

    def row(m, _):
        r = m + HALO
        x = tiles(r)
        taps = [
            mid[r - d],
            plus_ref[r - hi],
            shifted(x, 2 * d, False),
            minus_ref[r - hi],
            mid[r],
            plus_ref[r + lo],
            shifted(x, 2 * d, True),
            minus_ref[r + lo],
            mid[r + d],
        ]
        acc = lax.dot_general(
            weight,
            jnp.concatenate(taps, axis=0),
            (((1,), (0,)), ((), ())),
            preferred_element_type=jnp.float32,
        )
        acc = acc + bias
        if final:
            acc = acc + own_ref[m].astype(jnp.float32)
        else:
            acc = jnp.maximum(acc, 0.0)
        out_ref[m] = jnp.where(away <= threshold(limit_ref, row0 + m), acc, 0.0).astype(jnp.bfloat16)
        return 0

    lax.fori_loop(0, ROWS, row, 0, unroll=UNROLL)
    if final:
        mix(at_ref, limit_ref, out_ref, first_ref, second_ref, edge_ref, other_ref, plus_ref)
    else:
        pack_edges(out_ref, *edges)


def mix(at_ref, limit_ref, summed, first_ref, second_ref, edge_ref, other_ref, rows_ref):
    a = lax.broadcasted_iota(jnp.int32, (COLS, COLS), 0)
    b = lax.broadcasted_iota(jnp.int32, (COLS, COLS), 1)
    turn = (a + b == COLS).astype(jnp.bfloat16)
    lane = lax.broadcasted_iota(jnp.int32, (C, LANES), 1)
    away = both_offsets(at_ref[FOLD])
    row0 = at_ref[ROW]
    edges = [jnp.zeros((C, LANES), jnp.bfloat16)] * 2
    for group in range(ROWS // STACK):
        at = group * STACK
        cells = summed[pl.ds(at, STACK)].reshape(STACK * C, WIDE)
        blocks = cells[:, :COLS], cells[:, COLS:]
        turned = [jnp.dot(x, turn, preferred_element_type=jnp.float32) for x in blocks]
        for i in range(2):
            mean = 0.5 * (blocks[i].astype(jnp.float32) + turned[1 - i])
            for j in range(STACK):
                m = at + j
                part = slice(C * j, C * (j + 1))
                seen = away[:, COLS * i : COLS * (i + 1)] <= threshold(limit_ref, row0 + m)
                rows_ref[m, :, COLS * i : COLS * (i + 1)] = jnp.where(seen, mean[part], 0.0).astype(jnp.bfloat16)
                tile = blocks[i][part, :LANES]
                tile = pltpu.roll(tile, m, axis=1) if m else tile
                edges[i] = jnp.where(lane == m, tile, edges[i])
    swap = at_ref[CORE] == 0
    edge_ref[...] = jnp.where(swap, edges[1], edges[0])
    other_ref[...] = jnp.where(swap, edges[0], edges[1])
    early = at_ref[ORDER] == 0

    @pl.when(early)
    def _():
        first_ref[...] = jnp.swapaxes(rows_ref[pl.ds(0, ROWS), :, :COLS], 0, 1)
        second_ref[...] = jnp.swapaxes(rows_ref[pl.ds(0, ROWS), :, COLS:], 0, 1)

    @pl.when(jnp.logical_not(early))
    def _():
        first_ref[...] = jnp.swapaxes(rows_ref[pl.ds(0, ROWS), :, COLS:], 0, 1)
        second_ref[...] = jnp.swapaxes(rows_ref[pl.ds(0, ROWS), :, :COLS], 0, 1)


def conv(own, at, d, row_limit, cells, halos, weight, bias):
    final = own is not None
    in_specs = [SMEM] * 3 + [ANY] * 7 + [VMEM] * (3 if final else 2)
    args = [at, d, row_limit, cells, *halos, weight, bias] + ([own] if final else [])
    scratch = [pltpu.VMEM((ROWS, C, WIDE), jnp.bfloat16)] if final else []
    out_shape = [shape(C, ROWS, COLS)] * 2 + [shape(C, LANES)] * 2 if final else [shape(ROWS, C, WIDE)] + EDGES
    return pl.pallas_call(
        functools.partial(conv_kernel, final),
        in_specs=in_specs,
        out_specs=[VMEM] * len(out_shape),
        out_shape=out_shape,
        scratch_shapes=scratch
        + [
            pltpu.VMEM((SPAN, C, WIDE), jnp.bfloat16),
            pltpu.VMEM((SPAN, C, LANES), jnp.bfloat16),
            pltpu.VMEM((SPAN, C, LANES), jnp.bfloat16),
            pltpu.VMEM((SPAN, C, WIDE), jnp.bfloat16),
            pltpu.VMEM((SPAN, C, WIDE), jnp.bfloat16),
            pltpu.SemaphoreType.DMA((9,)),
        ],
        compiler_params=PARAMS,
        cost_estimate=cost(25.0 if final else 20.0),
        name="second" if final else "first",
    )(*args)


def flat(weight):
    return jnp.transpose(weight, (1, 0, 2)).reshape(C, 9 * C)


def local(band_map, dilations, row_limit, weight_one, bias_one, weight_two, bias_two):
    at = whereabouts()
    vector = jnp.stack(at)
    early, late = routes(0), routes(1)

    first = enter(0, vector, row_limit, band_map, [])
    second = enter(1, vector, row_limit, band_map, [first])
    first = lax.ppermute(first, AXES, early)
    second = lax.ppermute(second, AXES, late)
    cells, *edges = pack(vector, first, second)
    halos = exchange(at, *edges)
    hidden, *edges = conv(
        None, vector, dilations[:1], row_limit, cells, halos, flat(weight_one), bias_one[:, None]
    )
    halos = exchange(at, *edges)
    first, second, edge, other = conv(
        cells, vector, dilations[1:], row_limit, hidden, halos, flat(weight_two), bias_two[:, None]
    )

    pos, off = lax.axis_index("pos"), lax.axis_index("off")
    here = lambda pairs: functools.reduce(jnp.logical_or, [(pos % 2 == s) & (off == b) for s, b in pairs])
    stays, relayed = here(STAY), here(VIA)
    leave, arrive = [], []
    for to, at_work in early:
        stored, block = to // 8, to % 8
        if (stored % 2, block) in VIA:
            via = device(stored // 2, *VIA[stored % 2, block])
            leave.append((at_work, via))
            arrive.append((via, to))
        elif at_work != to:
            leave.append((at_work, to))
    passed = lax.ppermute(first, AXES, leave)
    direct = lax.ppermute(second, AXES, [(b, a) for a, b in late])
    ended = lax.ppermute(passed, AXES, arrive)

    to_first = lambda core: [(place(s, f), home(s // 2, f + 1)) for s, f in CELLS if s % 2 == core]
    to_second = lambda core: [(place(s, f), home(s // 2, 8 - f)) for s, f in CELLS if s % 2 == core and f]
    edge = lax.ppermute(edge, AXES, to_first(0) + to_second(1))
    other = lax.ppermute(other, AXES, to_second(0) + to_first(1))
    low = off <= 4
    top_edge, bottom_edge = jnp.where(low, edge, other), jnp.where(low, other, edge)

    got = jnp.where(stays, first, jnp.where(relayed, ended, passed))
    top_first = vector[EARLY] == 0
    column = lax.broadcasted_iota(jnp.int32, (1, 1, COLS), 2)

    def whole(cells, edge):
        more = cells.astype(jnp.float32) + 0.5 * edge[:, :ROWS, None].astype(jnp.float32)
        return jnp.where(column == 0, more.astype(jnp.bfloat16), cells)

    return jnp.concatenate(
        [
            whole(jnp.where(top_first, got, direct), top_edge),
            whole(jnp.where(top_first, direct, got), bottom_edge),
        ],
        axis=1,
    )


def solution(mesh):
    in_specs = (P(None, "pos", "off"), P(), P(), P(), P(), P(), P())
    out_specs = P(None, "pos", "off")
    return jax.shard_map(local, mesh=mesh, in_specs=in_specs, out_specs=out_specs, check_vma=False)
```

```python
import functools

import jax
import jax.numpy as jnp
from jax import lax
from jax.experimental import pallas as pl
from jax.experimental.pallas import tpu as pltpu
from jax.sharding import PartitionSpec as P

BAND = 1024
DMAX = 32
C = 48
ROWS = 72
COLS = 256
WIDE = 2 * COLS
LANES = 128
HALO = DMAX
CORNER = DMAX // 2
CHUNK = 24
PARTS = ((0, 24), (24, 48))
PREP = 8
UNROLL = 8
STACK = 8
AXES = ("pos", "off")

SMEM = pl.BlockSpec(memory_space=pltpu.SMEM)
VMEM = pl.BlockSpec(memory_space=pltpu.VMEM)
ANY = pl.BlockSpec(memory_space=pl.ANY)
HBM = pl.BlockSpec(memory_space=pltpu.HBM)
PARAMS = pltpu.CompilerParams(vmem_limit_bytes=63 * 2**20)


def device(pair, x, z, core):
    return (2 * pair + core) * 8 + 2 * z + x


def home(stored, block):
    return device(stored // 2, block % 2, block // 2, stored % 2)


def place(strip, fold):
    stored = strip // 2
    return device(stored // 2, stored % 2, (4 - fold) % 4, strip % 2)


def lead(stored, fold):
    return (fold == 1) & (stored % 2 == 0) | (fold == 3) & (stored % 2 == 1)


CELLS = [(strip, fold) for strip in range(32) for fold in range(4)]


def routes(turn):
    out = []
    for strip, fold in CELLS:
        core, stored = strip % 2, strip // 2
        first = (core == int(lead(stored, fold))) == (turn == 0)
        out.append((home(stored, fold if first else 7 - fold), place(strip, fold)))
    return out


VIA = {(0, 1): (0, 0, 0), (0, 7): (0, 3, 0), (1, 2): (1, 1, 1), (1, 4): (1, 2, 1)}
STAY = ((0, 0), (0, 6), (1, 3), (1, 5))


def moves(strip_step, fold_step):
    return [
        (place(s, f), place(s + strip_step, f + fold_step))
        for s, f in CELLS
        if 0 <= s + strip_step < 32 and 0 <= f + fold_step < 4
    ]


def whereabouts():
    pos, off = lax.axis_index("pos"), lax.axis_index("off")
    fold = jnp.minimum(off, 7 - off)
    early = jnp.where(off < 4, 0, 1) ^ lead(pos, fold).astype(jnp.int32)
    stored = 2 * (pos // 2) + off % 2
    core = pos % 2
    work = (4 - off // 2) % 4
    order = core ^ lead(stored, work).astype(jnp.int32)
    values = (pos * 2 * ROWS, off, early, stored * 2 * ROWS + core * ROWS, work, order, core)
    return [v.astype(jnp.int32) for v in values]


STORED_ROW, STORED_BLOCK, EARLY, ROW, FOLD, ORDER, CORE = range(7)


def threshold(limit_ref, row):
    last = limit_ref.shape[0] - 1
    return jnp.minimum(limit_ref[row], jnp.minimum(2 * row + 1, 2 * last - 2 * row))


def offsets(block, dims):
    return jnp.abs(lax.broadcasted_iota(jnp.int32, dims, len(dims) - 1) + (block * COLS - BAND))


def both_offsets(fold):
    return jnp.concatenate([offsets(fold, (C, COLS)), offsets(7 - fold, (C, COLS))], axis=1)


def shape(*dims):
    return jax.ShapeDtypeStruct(dims, jnp.bfloat16)


def enter_kernel(turn, at_ref, limit_ref, x_ref, out_ref):
    x = jnp.swapaxes(x_ref[...], 0, 1)
    away = offsets(at_ref[STORED_BLOCK], (C, COLS))
    row0 = at_ref[STORED_ROW] + (at_ref[EARLY] ^ turn) * ROWS
    for i in range(ROWS):
        seen = away <= threshold(limit_ref, row0 + i)
        out_ref[i] = jnp.where(seen, x[i], jnp.zeros((), jnp.bfloat16))


def enter(turn, at, row_limit, band_map):
    return pl.pallas_call(
        functools.partial(enter_kernel, turn),
        grid_spec=pltpu.PrefetchScalarGridSpec(
            num_scalar_prefetch=1,
            grid=(1,),
            in_specs=[SMEM, pl.BlockSpec((C, ROWS, COLS), lambda i, at_ref: (0, at_ref[EARLY] ^ turn, 0))],
            out_specs=pl.BlockSpec((ROWS, C, COLS), lambda i, at_ref: (0, 0, 0)),
        ),
        out_shape=shape(ROWS, C, COLS),
        compiler_params=PARAMS,
        name="enter",
    )(at, row_limit, band_map)


EDGES = [shape(ROWS, C, LANES)] * 2 + [shape(HALO, C, WIDE)] * 2


def edge_copies(cells, first, count, top, bottom):
    out = []
    for target, at in ((top, 0), (bottom, ROWS - HALO)):
        low, high = max(first, at), min(first + count, at + HALO)
        if low < high:
            out.append((cells.at[pl.ds(low - first, high - low)], target.at[pl.ds(low - at, high - low)]))
    return out


def inward_outward(cells, lane):
    return (
        jnp.where(lane < 64, cells[:, 2 * LANES : 3 * LANES], cells[:, LANES : 2 * LANES]),
        jnp.where(lane < 64, cells[:, :LANES], cells[:, 3 * LANES :]),
    )


def pack_kernel(at_ref, early_ref, late_ref, *refs):
    out_ref, inward, outward, top, bottom, blocks, into, back, sems = refs[-9:]
    lane = lax.broadcasted_iota(jnp.int32, (C, LANES), 1)
    runs = [pl.ds(i, CHUNK) for i in range(0, ROWS, CHUNK)]

    def work(first, second):
        n = 0

        def copy(src, dst):
            nonlocal n
            n += 1
            made = pltpu.make_async_copy(src, dst, sems.at[n - 1])
            made.start()
            return made

        here = [[copy(x.at[run], blocks.at[i, run]) for i, x in enumerate((first, second))] for run in runs]
        sent = []
        for at, run, loads in zip(range(0, ROWS, CHUNK), runs, here):
            for load in loads:
                load.wait()
            for i in range(at, at + CHUNK):
                a, b = blocks[0, i], blocks[1, i]
                into[i] = jnp.where(lane < 64, b[:, :LANES], a[:, LANES:])
                back[i] = jnp.where(lane < 64, a[:, :LANES], b[:, LANES:])
            sent += [copy(into.at[run], inward.at[run]), copy(back.at[run], outward.at[run])]
            for i in range(2):
                lanes = pl.ds(i * COLS, COLS)
                pairs = [(blocks.at[i, run], out_ref.at[run, :, lanes])]
                for src, dst in edge_copies(blocks.at[i, run], at, CHUNK, top, bottom):
                    pairs.append((src, dst.at[:, :, lanes]))
                sent += [copy(src, dst) for src, dst in pairs]
        for done in sent:
            done.wait()

    @pl.when(at_ref[ORDER] == 0)
    def _():
        work(early_ref, late_ref)

    @pl.when(at_ref[ORDER] != 0)
    def _():
        work(late_ref, early_ref)


def pack(at, early, late, after):
    out = [shape(ROWS, C, WIDE)] + EDGES
    return pl.pallas_call(
        pack_kernel,
        in_specs=[SMEM] + [ANY] * (2 + len(after)),
        out_specs=[HBM] * len(out),
        out_shape=out,
        scratch_shapes=[
            pltpu.VMEM((2, ROWS, C, COLS), jnp.bfloat16),
            pltpu.VMEM((ROWS, C, LANES), jnp.bfloat16),
            pltpu.VMEM((ROWS, C, LANES), jnp.bfloat16),
            pltpu.SemaphoreType.DMA((32,)),
        ],
        compiler_params=PARAMS,
        name="pack",
    )(at, early, late, *after)


def send(cells, strip_step, fold_step):
    return lax.ppermute(cells, AXES, moves(strip_step, fold_step))


def exchange(at, inward, outward, top, bottom):
    previous = send(inward, 0, 1)
    following = send(outward, 0, -1)
    below = send(top, -1, 0)
    above = send(bottom, 1, 0)
    following = jnp.where(at[FOLD] == 3, inward, following)
    ends = lambda first: jnp.concatenate(
        [lax.slice_in_dim(x, first, first + CORNER) for x in (previous, following)], axis=0
    )
    corner_below = send(ends(0), -1, 0)
    corner_above = send(ends(ROWS - CORNER), 1, 0)
    return previous, following, above, below, corner_above, corner_below


def conv_kernel(which, first, count, extra, at_ref, d_ref, limit_ref, cells, *refs):
    final = which == 1
    previous, following, above, below, corner_above, corner_below, w_ref, b_ref = refs[:8]
    refs = refs[8:]
    if final:
        own_ref, carried, refs = refs[0], refs[1 : 1 + extra], refs[1 + extra :]
        outs, scratch = refs[:4], refs[4:]
        out_ref, own, mid, before, behind, plus_ref, minus_ref, sems = scratch
    else:
        outs, scratch = refs[:5], refs[5:]
        out_ref, in_ref, back_ref, mid, before, behind, plus_ref, minus_ref, sems = scratch

    base = first - HALO
    started = []

    def fetch(src, low, high, target, shift):
        low, high = max(low, base), min(high, first + count + HALO)
        if low < high:
            started.append(
                pltpu.make_async_copy(
                    src.at[pl.ds(low - shift, high - low)],
                    target.at[pl.ds(low - base, high - low)],
                    sems.at[len(started)],
                )
            )

    fetch(above, -HALO, 0, mid, -HALO)
    fetch(corner_above, -CORNER, 0, before, -CORNER)
    fetch(corner_above, -CORNER, 0, behind, -2 * CORNER)
    fetch(cells, 0, ROWS, mid, 0)
    fetch(previous, 0, ROWS, before, 0)
    fetch(following, 0, ROWS, behind, 0)
    fetch(below, ROWS, ROWS + HALO, mid, ROWS)
    fetch(corner_below, ROWS, ROWS + CORNER, before, ROWS)
    fetch(corner_below, ROWS, ROWS + CORNER, behind, ROWS - CORNER)
    if final:
        late = pltpu.make_async_copy(own_ref.at[pl.ds(first, count)], own, sems.at[len(started)])
    for copy in started:
        copy.start()
    if final:
        late.start()
    for copy in started:
        copy.wait()

    d = d_ref[which]
    lo = d // 2
    hi = (d + 1) // 2
    odd = d - 2 * lo
    lane = lax.broadcasted_iota(jnp.int32, (C, LANES), 1)
    even_lane = (lane & 1) == 0

    def tiles(r):
        own = [mid[r, :, LANES * i : LANES * (i + 1)] for i in range(4)]
        return [before[r], *own[:2], behind[r], *own[2:]]

    def shifted(t, step, back):
        keep = lane < (step if back else LANES - step)
        turn = step if back else LANES - step
        left, a, b, right, c, e = t
        runs = ((left, a, b), (right, c, e)) if back else ((a, b, right), (c, e, left))
        out = []
        for run in runs:
            x, y, z = [pltpu.roll(v, turn, axis=1) for v in run]
            out += [jnp.where(keep, x, y), jnp.where(keep, y, z)]
        return jnp.concatenate(out, axis=1)

    start = HALO - hi

    def prepare(i, _):
        for j in range(PREP):
            r = start + i * PREP + j
            x, y = tiles(r), tiles(r + odd)
            both = [jnp.where(even_lane, b, a) for a, b in zip(x, y)]
            plus_ref[r] = shifted(both, d, False)
            minus_ref[r] = shifted(both, d, True)
        return 0

    lax.fori_loop(0, (count + d + PREP - 1) // PREP, prepare, 0)

    if final:
        late.wait()
    weight = w_ref[...]
    bias = b_ref[...]
    away = both_offsets(at_ref[FOLD])
    row0 = at_ref[ROW] + first

    def row(m, _):
        r = m + HALO
        x = tiles(r)
        taps = [
            mid[r - d],
            plus_ref[r - hi],
            shifted(x, 2 * d, False),
            minus_ref[r - hi],
            mid[r],
            plus_ref[r + lo],
            shifted(x, 2 * d, True),
            minus_ref[r + lo],
            mid[r + d],
        ]
        acc = lax.dot_general(
            weight,
            jnp.concatenate(taps, axis=0),
            (((1,), (0,)), ((), ())),
            preferred_element_type=jnp.float32,
        )
        acc = acc + bias
        if final:
            acc = acc + own[m].astype(jnp.float32)
        else:
            acc = jnp.maximum(acc, 0.0)
        acc = jnp.where(away <= threshold(limit_ref, row0 + m), acc, 0.0).astype(jnp.bfloat16)
        out_ref[m] = acc
        if not final:
            in_ref[m], back_ref[m] = inward_outward(acc, lane)
        return 0

    if final:
        lax.fori_loop(0, count, row, 0, unroll=UNROLL)
        mix(at_ref, limit_ref, first, count, out_ref, carried, *outs, plus_ref)
        return
    hidden, into, back, top, bottom = outs
    copies = []
    for at in range(0, ROWS, CHUNK):
        lax.fori_loop(at, at + CHUNK, row, 0, unroll=UNROLL)
        run = pl.ds(at, CHUNK)
        pairs = [(a.at[run], b.at[run]) for a, b in ((out_ref, hidden), (in_ref, into), (back_ref, back))]
        pairs += edge_copies(out_ref.at[run], at, CHUNK, top, bottom)
        for a, b in pairs:
            copies.append(pltpu.make_async_copy(a, b, sems.at[len(started) + len(copies)]))
            copies[-1].start()
    for copy in copies:
        copy.wait()


def mix(at_ref, limit_ref, first, count, summed, carried, first_ref, second_ref, edge_ref, other_ref, rows_ref):
    a = lax.broadcasted_iota(jnp.int32, (COLS, COLS), 0)
    b = lax.broadcasted_iota(jnp.int32, (COLS, COLS), 1)
    turn = (a + b == COLS).astype(jnp.bfloat16)
    lane = lax.broadcasted_iota(jnp.int32, (C, LANES), 1)
    away = both_offsets(at_ref[FOLD])
    row0 = at_ref[ROW] + first
    swap = at_ref[CORE] == 0
    edges = [jnp.zeros((C, LANES), jnp.bfloat16)] * 2
    if carried:
        edge, other = carried[0][...], carried[1][...]
        edges = [jnp.where(swap, other, edge), jnp.where(swap, edge, other)]
    for group in range(count // STACK):
        at = group * STACK
        cells = summed[pl.ds(at, STACK)].reshape(STACK * C, WIDE)
        blocks = cells[:, :COLS], cells[:, COLS:]
        turned = [jnp.dot(x, turn, preferred_element_type=jnp.float32) for x in blocks]
        for i in range(2):
            mean = 0.5 * (blocks[i].astype(jnp.float32) + turned[1 - i])
            for j in range(STACK):
                m = at + j
                part = slice(C * j, C * (j + 1))
                seen = away[:, COLS * i : COLS * (i + 1)] <= threshold(limit_ref, row0 + m)
                rows_ref[m, :, COLS * i : COLS * (i + 1)] = jnp.where(seen, mean[part], 0.0).astype(jnp.bfloat16)
                tile = blocks[i][part, :LANES]
                tile = pltpu.roll(tile, first + m, axis=1) if first + m else tile
                edges[i] = jnp.where(lane == first + m, tile, edges[i])
    edge_ref[...] = jnp.where(swap, edges[1], edges[0])
    other_ref[...] = jnp.where(swap, edges[0], edges[1])
    early = at_ref[ORDER] == 0

    @pl.when(early)
    def _():
        first_ref[...] = jnp.swapaxes(rows_ref[pl.ds(0, count), :, :COLS], 0, 1)
        second_ref[...] = jnp.swapaxes(rows_ref[pl.ds(0, count), :, COLS:], 0, 1)

    @pl.when(jnp.logical_not(early))
    def _():
        first_ref[...] = jnp.swapaxes(rows_ref[pl.ds(0, count), :, COLS:], 0, 1)
        second_ref[...] = jnp.swapaxes(rows_ref[pl.ds(0, count), :, :COLS], 0, 1)


def conv(own, at, d, row_limit, cells, halos, weight, bias, rows=(0, ROWS), carried=()):
    final = own is not None
    first, count = rows
    span = count + 2 * HALO
    in_specs = [SMEM] * 3 + [ANY] * 7 + [VMEM] * 2 + [ANY] * int(final) + [VMEM] * len(carried)
    args = [at, d, row_limit, cells, *halos, weight, bias] + ([own] if final else []) + list(carried)
    out_shape = [shape(C, count, COLS)] * 2 + [shape(C, LANES)] * 2 if final else [shape(ROWS, C, WIDE)] + EDGES
    scratch = [pltpu.VMEM((count, C, n), jnp.bfloat16) for n in ((WIDE, WIDE) if final else (WIDE, LANES, LANES))]
    return pl.pallas_call(
        functools.partial(conv_kernel, int(final), first, count, len(carried)),
        in_specs=in_specs,
        out_specs=[VMEM if final else HBM] * len(out_shape),
        out_shape=out_shape,
        scratch_shapes=scratch
        + [pltpu.VMEM((span, C, n), jnp.bfloat16) for n in (WIDE, LANES, LANES, WIDE, WIDE)]
        + [pltpu.SemaphoreType.DMA((32,))],
        compiler_params=PARAMS,
        name="second" if final else "first",
    )(*args)


def behind_kernel(*refs):
    del refs


def behind(cells, others):
    return pl.pallas_call(
        behind_kernel,
        in_specs=[ANY] * (len(cells) + len(others)),
        out_specs=[ANY] * len(cells),
        out_shape=[shape(*x.shape) for x in cells],
        input_output_aliases={i: i for i in range(len(cells))},
        compiler_params=PARAMS,
        name="behind",
    )(*cells, *others)


def flat(weight):
    return jnp.transpose(weight, (1, 0, 2)).reshape(C, 9 * C)


def local(band_map, dilations, row_limit, weight_one, bias_one, weight_two, bias_two):
    at = whereabouts()
    vector = jnp.stack(at)
    early, late = routes(0), routes(1)

    first = lax.ppermute(enter(0, vector, row_limit, band_map), AXES, early)
    second = lax.ppermute(enter(1, vector, row_limit, band_map), AXES, late)
    weights = [flat(weight_one), flat(weight_two)]
    biases = [bias_one[:, None], bias_two[:, None]]
    cells, *edges = pack(vector, first, second, weights + biases)
    halos = exchange(at, *edges)
    hidden, *edges = conv(None, vector, dilations, row_limit, cells, halos, weights[0], biases[0])
    halos = exchange(at, *edges)

    pos, off = lax.axis_index("pos"), lax.axis_index("off")
    here = lambda pairs: functools.reduce(jnp.logical_or, [(pos % 2 == s) & (off == b) for s, b in pairs])
    stays, relayed = here(STAY), here(VIA)
    leave, arrive = [], []
    for to, at_work in early:
        stored, block = to // 8, to % 8
        if (stored % 2, block) in VIA:
            via = device(stored // 2, *VIA[stored % 2, block])
            leave.append((at_work, via))
            arrive.append((via, to))
        elif at_work != to:
            leave.append((at_work, to))

    gots, directs, sent, carried = [], [], (), []
    for rows in PARTS:
        first, second, *carried = conv(
            cells, vector, dilations, row_limit, hidden, halos, weights[1], biases[1], rows, carried
        )
        if sent:
            first, second, *carried = behind((first, second, *carried), sent)
        passed = lax.ppermute(first, AXES, leave)
        directs.append(lax.ppermute(second, AXES, [(b, a) for a, b in late]))
        ended = lax.ppermute(passed, AXES, arrive)
        gots.append(jnp.where(stays, first, jnp.where(relayed, ended, passed)))
        sent = (passed, directs[-1])
    edge, other = carried

    to_first = lambda core: [(place(s, f), home(s // 2, f + 1)) for s, f in CELLS if s % 2 == core]
    to_second = lambda core: [(place(s, f), home(s // 2, 8 - f)) for s, f in CELLS if s % 2 == core and f]
    edge = lax.ppermute(edge, AXES, to_first(0) + to_second(1))
    other = lax.ppermute(other, AXES, to_second(0) + to_first(1))
    low = at[STORED_BLOCK] <= 4
    halves = jnp.where(low, edge, other), jnp.where(low, other, edge)
    top_first = at[EARLY] == 0
    column = lax.broadcasted_iota(jnp.int32, (1, 1, COLS), 2)
    out = []
    for half in range(2):
        for (start, count), *pair in zip(PARTS, gots, directs):
            got = jnp.where(top_first, *(pair if half == 0 else pair[::-1]))
            edge = lax.slice_in_dim(halves[half], start, start + count, axis=1)[:, :, None]
            more = (got.astype(jnp.float32) + 0.5 * edge.astype(jnp.float32)).astype(jnp.bfloat16)
            out.append(jnp.where(column == 0, more, got))
    return jnp.concatenate(out, axis=1)


def solution(mesh):
    in_specs = (P(None, "pos", "off"), P(), P(), P(), P(), P(), P())
    out_specs = P(None, "pos", "off")
    return jax.shard_map(local, mesh=mesh, in_specs=in_specs, out_specs=out_specs, check_vma=False)
```

```python
import functools

import jax
import jax.numpy as jnp
from jax import lax
from jax.experimental import pallas as pl
from jax.experimental.pallas import tpu as pltpu
from jax.sharding import PartitionSpec as P

BAND = 1024
DMAX = 32
C = 48
ROWS = 72
COLS = 256
WIDE = 2 * COLS
LANES = 128
HALO = DMAX
CORNER = DMAX // 2
CHUNK = 24
PARTS = (((0, 24),), ((24, 48),))
PREP = 8
UNROLL = 8
STACK = 8
AXES = ("pos", "off")

SMEM = pl.BlockSpec(memory_space=pltpu.SMEM)
VMEM = pl.BlockSpec(memory_space=pltpu.VMEM)
ANY = pl.BlockSpec(memory_space=pl.ANY)
HBM = pl.BlockSpec(memory_space=pltpu.HBM)
PARAMS = pltpu.CompilerParams(vmem_limit_bytes=63 * 2**20)


def device(pair, x, z, core):
    return (2 * pair + core) * 8 + 2 * z + x


def home(stored, block):
    return device(stored // 2, block % 2, block // 2, stored % 2)


def place(strip, fold):
    stored = strip // 2
    return device(stored // 2, stored % 2, (4 - fold) % 4, strip % 2)


def lead(stored, fold):
    return (fold == 1) & (stored % 2 == 0) | (fold == 3) & (stored % 2 == 1)


CELLS = [(strip, fold) for strip in range(32) for fold in range(4)]


def routes(turn):
    out = []
    for strip, fold in CELLS:
        core, stored = strip % 2, strip // 2
        first = (core == int(lead(stored, fold))) == (turn == 0)
        out.append((home(stored, fold if first else 7 - fold), place(strip, fold)))
    return out


VIA = {(0, 1): (0, 0, 0), (0, 7): (0, 3, 0), (1, 2): (1, 1, 1), (1, 4): (1, 2, 1)}
STAY = ((0, 0), (0, 6), (1, 3), (1, 5))


def whereabouts():
    pos, off = lax.axis_index("pos"), lax.axis_index("off")
    fold = jnp.minimum(off, 7 - off)
    early = jnp.where(off < 4, 0, 1) ^ lead(pos, fold).astype(jnp.int32)
    stored = 2 * (pos // 2) + off % 2
    core = pos % 2
    work = (4 - off // 2) % 4
    order = core ^ lead(stored, work).astype(jnp.int32)
    values = (pos * 2 * ROWS, off, early, stored * 2 * ROWS + core * ROWS, work, order, core)
    values += (jnp.where(work == 3, 2, work % 2), core + 2 * (work % 2))
    return [v.astype(jnp.int32) for v in values]


STORED_ROW, STORED_BLOCK, EARLY, ROW, FOLD, ORDER, CORE, SIDE, KIND = range(9)


def choose(at_ref, index, cases):
    for value, case in enumerate(cases):
        pl.when(at_ref[index] == value)(case)


def threshold(limit_ref, row):
    last = limit_ref.shape[0] - 1
    return jnp.minimum(limit_ref[row], jnp.minimum(2 * row + 1, 2 * last - 2 * row))


def offsets(block, dims):
    return jnp.abs(lax.broadcasted_iota(jnp.int32, dims, len(dims) - 1) + (block * COLS - BAND))


def both_offsets(fold):
    return jnp.concatenate([offsets(fold, (C, COLS)), offsets(7 - fold, (C, COLS))], axis=1)


def shape(*dims):
    return jax.ShapeDtypeStruct(dims, jnp.bfloat16)


def enter_kernel(turn, at_ref, limit_ref, x_ref, out_ref):
    x = jnp.swapaxes(x_ref[...], 0, 1)
    away = offsets(at_ref[STORED_BLOCK], (C, COLS))
    row0 = at_ref[STORED_ROW] + (at_ref[EARLY] ^ turn) * ROWS
    for i in range(ROWS):
        seen = away <= threshold(limit_ref, row0 + i)
        out_ref[i] = jnp.where(seen, x[i], jnp.zeros((), jnp.bfloat16))


def enter(turn, at, row_limit, band_map):
    return pl.pallas_call(
        functools.partial(enter_kernel, turn),
        grid_spec=pltpu.PrefetchScalarGridSpec(
            num_scalar_prefetch=1,
            grid=(1,),
            in_specs=[SMEM, pl.BlockSpec((C, ROWS, COLS), lambda i, at_ref: (0, at_ref[EARLY] ^ turn, 0))],
            out_specs=pl.BlockSpec((ROWS, C, COLS), lambda i, at_ref: (0, 0, 0)),
        ),
        out_shape=shape(ROWS, C, COLS),
        compiler_params=PARAMS,
        name="enter",
    )(at, row_limit, band_map)


EDGES = [shape(ROWS, C, LANES)] * 2 + [shape(HALO, C, WIDE)] * 2


def edge_copies(cells, first, count, top, bottom):
    out = []
    for target, at in ((top, 0), (bottom, ROWS - HALO)):
        low, high = max(first, at), min(first + count, at + HALO)
        if low < high:
            out.append((cells.at[pl.ds(low - first, high - low)], target.at[pl.ds(low - at, high - low)]))
    return out


def inward_outward(cells, lane):
    return (
        jnp.where(lane < 64, cells[:, 2 * LANES : 3 * LANES], cells[:, LANES : 2 * LANES]),
        jnp.where(lane < 64, cells[:, :LANES], cells[:, 3 * LANES :]),
    )


def pack_kernel(at_ref, early_ref, late_ref, *refs):
    near, far, mate, other, blocks, into, back, sems = refs[-8:]
    lane = lax.broadcasted_iota(jnp.int32, (C, LANES), 1)
    runs = [pl.ds(i, CHUNK) for i in range(0, ROWS, CHUNK)]

    def work(first, second, inward, outward, top, bottom):
        n = 0

        def copy(src, dst):
            nonlocal n
            n += 1
            made = pltpu.make_async_copy(src, dst, sems.at[n - 1])
            made.start()
            return made

        here = [[copy(x.at[run], blocks.at[i, run]) for i, x in enumerate((first, second))] for run in runs]
        sent = []
        for at, run, loads in zip(range(0, ROWS, CHUNK), runs, here):
            for load in loads:
                load.wait()
            for i in range(at, at + CHUNK):
                a, b = blocks[0, i], blocks[1, i]
                into[i] = jnp.where(lane < 64, b[:, :LANES], a[:, LANES:])
                back[i] = jnp.where(lane < 64, a[:, :LANES], b[:, LANES:])
            sent += [copy(into.at[run], inward.at[run]), copy(back.at[run], outward.at[run])]
            for i in range(2):
                lanes = pl.ds(i * COLS, COLS)
                for src, dst in edge_copies(blocks.at[i, run], at, CHUNK, top, bottom):
                    sent.append(copy(src, dst.at[:, :, lanes]))
        for done in sent:
            done.wait()

    for order in range(2):

        def case(kind):
            cells = (late_ref, early_ref) if order else (early_ref, late_ref)
            edges = (far, near) if kind // 2 else (near, far)
            rows = (mate, other) if kind % 2 else (other, mate)
            return lambda: work(*cells, *edges, *rows)

        @pl.when(at_ref[ORDER] == order)
        def _():
            choose(at_ref, KIND, [case(kind) for kind in range(4)])


def pack(at, early, late, after):
    return pl.pallas_call(
        pack_kernel,
        in_specs=[SMEM] + [ANY] * (2 + len(after)),
        out_specs=[HBM] * 4,
        out_shape=EDGES,
        scratch_shapes=[
            pltpu.VMEM((2, ROWS, C, COLS), jnp.bfloat16),
            pltpu.VMEM((ROWS, C, LANES), jnp.bfloat16),
            pltpu.VMEM((ROWS, C, LANES), jnp.bfloat16),
            pltpu.SemaphoreType.DMA((96,)),
        ],
        compiler_params=PARAMS,
        name="pack",
    )(at, early, late, *after)


MATES = [(place(s, f), place(s ^ 1, f)) for s, f in CELLS]
OTHERS = [(place(s, f), place(t, f)) for s, f in CELLS for t in [s + 1 if s % 2 else s - 1] if 0 <= t < 32]
NEAR = [(place(s, f), place(s, f ^ 1)) for s, f in CELLS]
FAR = [(place(s, f), place(s, 3 - f)) for s, f in CELLS if f in (1, 2)]


def exchange(at, near, far, mate, other):
    beside = far
    near = lax.ppermute(near, AXES, NEAR)
    far = lax.ppermute(far, AXES, FAR)
    mate = lax.ppermute(mate, AXES, MATES)
    other = lax.ppermute(other, AXES, OTHERS)
    ends = lambda first: jnp.concatenate(
        [
            lax.dynamic_slice_in_dim(near, first, CORNER),
            jnp.where(at[FOLD] == 3, *[lax.dynamic_slice_in_dim(x, first, CORNER) for x in (beside, far)]),
        ],
        axis=0,
    )
    down = at[CORE] == 0
    corner_mate = lax.ppermute(ends(jnp.where(down, ROWS - CORNER, 0)), AXES, MATES)
    corner_other = lax.ppermute(ends(jnp.where(down, 0, ROWS - CORNER)), AXES, OTHERS)
    return (near, far, beside, mate, other), (corner_mate, corner_other)


def reach(runs):
    return runs[0][0] - HALO, sum(runs[-1]) + HALO


def needs_corners(runs):
    low, high = reach(runs)
    return low < CORNER - HALO or high > ROWS + HALO - CORNER


def conv_kernel(which, runs, extra, at_ref, d_ref, limit_ref, early_ref, late_ref, *refs):
    final = which == 1
    near, far, beside, mate, other, w_ref, b_ref = refs[:7]
    refs = refs[7:]
    if needs_corners(runs):
        (corner_mate, corner_other), refs = refs[:2], refs[2:]
    if final:
        hidden_ref, carried, refs = refs[0], refs[1 : 1 + extra], refs[1 + extra :]
        outs, scratch = refs[:4], refs[4:]
        out_ref, own, mid, before, behind, plus_ref, minus_ref, sems = scratch
    else:
        outs, scratch = refs[:5], refs[5:]
        out_ref, in_ref, back_ref, mid, before, behind, plus_ref, minus_ref, sems = scratch

    base, end = reach(runs)
    made = []

    def copy(src, dst):
        made.append(pltpu.make_async_copy(src, dst, sems.at[len(made)]))
        return made[-1]

    def fetch(src, low, high, target, shift):
        low, high = max(low, base), min(high, end)
        if low >= high:
            return []
        return [copy(src.at[pl.ds(low - shift, high - low)], target.at[pl.ds(low - base, high - low)])]

    def own_cells(low, count, target, at):
        rows, to = pl.ds(low, count), pl.ds(at, count)
        lanes = [pl.ds(i * COLS, COLS) for i in range(2)]
        return [
            [copy(x.at[rows], target.at[to, :, lane]) for x, lane in zip(pair, lanes)]
            for pair in ((early_ref, late_ref), (late_ref, early_ref))
        ]

    def each(choice, act):
        index, groups = choice

        def case(group):
            return lambda: [act(c) for c in group] and None

        choose(at_ref, index, [case(group) for group in groups])

    rows = [
        fetch(above, -HALO, 0, mid, -HALO) + fetch(below, ROWS, ROWS + HALO, mid, ROWS)
        for above, below in ((other, mate), (mate, other))
    ]
    sides = [
        fetch(near, 0, ROWS, a, 0) + fetch(x, 0, ROWS, b, 0)
        for a, b, x in ((behind, before, far), (before, behind, far), (before, behind, beside))
    ]
    choices = [(CORE, rows), (SIDE, sides)]
    if needs_corners(runs):
        ends = []
        for kind in range(4):
            above, below = (corner_mate, corner_other) if kind % 2 else (corner_other, corner_mate)
            a, b = (before, behind) if kind // 2 else (behind, before)
            ends.append(
                fetch(above, -CORNER, 0, a, -CORNER)
                + fetch(above, -CORNER, 0, b, -2 * CORNER)
                + fetch(below, ROWS, ROWS + CORNER, a, ROWS)
                + fetch(below, ROWS, ROWS + CORNER, b, ROWS - CORNER)
            )
        choices.append((KIND, ends))
    always = []
    later = []
    if final:
        always = fetch(hidden_ref, 0, ROWS, mid, 0)
        at = 0
        for first, count in runs:
            later.append((ORDER, own_cells(first, count, own, at)))
            at += count
    else:
        low, high = max(base, 0), min(end, ROWS)
        choices.append((ORDER, own_cells(low, high - low, mid, low - base)))
    for c in always:
        c.start()
    for choice in choices + later:
        each(choice, lambda c: c.start())
    for c in always:
        c.wait()
    for choice in choices:
        each(choice, lambda c: c.wait())

    d = d_ref[which]
    lo = d // 2
    hi = (d + 1) // 2
    odd = d - 2 * lo
    lane = lax.broadcasted_iota(jnp.int32, (C, LANES), 1)
    even_lane = (lane & 1) == 0

    def tiles(r):
        own = [mid[r, :, LANES * i : LANES * (i + 1)] for i in range(4)]
        return [before[r], *own[:2], behind[r], *own[2:]]

    def shifted(t, step, back):
        keep = lane < (step if back else LANES - step)
        turn = step if back else LANES - step
        left, a, b, right, c, e = t
        runs = ((left, a, b), (right, c, e)) if back else ((a, b, right), (c, e, left))
        out = []
        for run in runs:
            x, y, z = [pltpu.roll(v, turn, axis=1) for v in run]
            out += [jnp.where(keep, x, y), jnp.where(keep, y, z)]
        return jnp.concatenate(out, axis=1)

    for first, count in runs:
        start = first - base - hi

        def prepare(i, _):
            for j in range(PREP):
                r = start + i * PREP + j
                x, y = tiles(r), tiles(r + odd)
                both = [jnp.where(even_lane, b, a) for a, b in zip(x, y)]
                plus_ref[r] = shifted(both, d, False)
                minus_ref[r] = shifted(both, d, True)
            return 0

        lax.fori_loop(0, (count + d + PREP - 1) // PREP, prepare, 0)

    for choice in later:
        each(choice, lambda c: c.wait())
    weight = w_ref[...]
    bias = b_ref[...]
    away = both_offsets(at_ref[FOLD])
    row0 = at_ref[ROW]

    def row(ahead, m, _):
        r = m + ahead - base
        x = tiles(r)
        taps = [
            mid[r - d],
            plus_ref[r - hi],
            shifted(x, 2 * d, False),
            minus_ref[r - hi],
            mid[r],
            plus_ref[r + lo],
            shifted(x, 2 * d, True),
            minus_ref[r + lo],
            mid[r + d],
        ]
        acc = lax.dot_general(
            weight,
            jnp.concatenate(taps, axis=0),
            (((1,), (0,)), ((), ())),
            preferred_element_type=jnp.float32,
        )
        acc = acc + bias
        if final:
            acc = acc + own[m].astype(jnp.float32)
        else:
            acc = jnp.maximum(acc, 0.0)
        acc = jnp.where(away <= threshold(limit_ref, row0 + ahead + m), acc, 0.0).astype(jnp.bfloat16)
        out_ref[m] = acc
        if not final:
            in_ref[m], back_ref[m] = inward_outward(acc, lane)
        return 0

    if final:
        at = 0
        for first, count in runs:
            lax.fori_loop(at, at + count, functools.partial(row, first - at), 0, unroll=UNROLL)
            at += count
        mix(at_ref, limit_ref, runs, out_ref, carried, *outs, plus_ref)
        return
    hidden, to_near, to_far, to_mate, to_other = outs
    copies, ways = [], [[] for _ in range(4)]
    for at in range(0, ROWS, CHUNK):
        lax.fori_loop(at, at + CHUNK, functools.partial(row, 0), 0, unroll=UNROLL)
        run = pl.ds(at, CHUNK)
        copies.append(copy(out_ref.at[run], hidden.at[run]))
        copies[-1].start()
        more = []
        for kind in range(4):
            top, bottom = (to_mate, to_other) if kind % 2 else (to_other, to_mate)
            inward, outward = (to_far, to_near) if kind // 2 else (to_near, to_far)
            pairs = [(in_ref.at[run], inward.at[run]), (back_ref.at[run], outward.at[run])]
            pairs += edge_copies(out_ref.at[run], at, CHUNK, top, bottom)
            more.append([copy(a, b) for a, b in pairs])
        each((KIND, more), lambda c: c.start())
        for way, group in zip(ways, more):
            way += group
    for c in copies:
        c.wait()
    each((KIND, ways), lambda c: c.wait())


def mix(at_ref, limit_ref, runs, summed, carried, first_ref, second_ref, edge_ref, other_ref, rows_ref):
    a = lax.broadcasted_iota(jnp.int32, (COLS, COLS), 0)
    b = lax.broadcasted_iota(jnp.int32, (COLS, COLS), 1)
    turn = (a + b == COLS).astype(jnp.bfloat16)
    lane = lax.broadcasted_iota(jnp.int32, (C, LANES), 1)
    away = both_offsets(at_ref[FOLD])
    row0 = at_ref[ROW]
    rows = [first + i for first, count in runs for i in range(count)]
    swap = at_ref[CORE] == 0
    edges = [jnp.zeros((C, LANES), jnp.bfloat16)] * 2
    if carried:
        edge, other = carried[0][...], carried[1][...]
        edges = [jnp.where(swap, other, edge), jnp.where(swap, edge, other)]
    for group in range(len(rows) // STACK):
        at = group * STACK
        cells = summed[pl.ds(at, STACK)].reshape(STACK * C, WIDE)
        blocks = cells[:, :COLS], cells[:, COLS:]
        turned = [jnp.dot(x, turn, preferred_element_type=jnp.float32) for x in blocks]
        for i in range(2):
            mean = 0.5 * (blocks[i].astype(jnp.float32) + turned[1 - i])
            for j in range(STACK):
                m = at + j
                part = slice(C * j, C * (j + 1))
                seen = away[:, COLS * i : COLS * (i + 1)] <= threshold(limit_ref, row0 + rows[m])
                rows_ref[m, :, COLS * i : COLS * (i + 1)] = jnp.where(seen, mean[part], 0.0).astype(jnp.bfloat16)
                tile = blocks[i][part, :LANES]
                tile = pltpu.roll(tile, rows[m], axis=1) if rows[m] else tile
                edges[i] = jnp.where(lane == rows[m], tile, edges[i])
    edge_ref[...] = jnp.where(swap, edges[1], edges[0])
    other_ref[...] = jnp.where(swap, edges[0], edges[1])
    early = at_ref[ORDER] == 0

    @pl.when(early)
    def _():
        first_ref[...] = jnp.swapaxes(rows_ref[pl.ds(0, len(rows)), :, :COLS], 0, 1)
        second_ref[...] = jnp.swapaxes(rows_ref[pl.ds(0, len(rows)), :, COLS:], 0, 1)

    @pl.when(jnp.logical_not(early))
    def _():
        first_ref[...] = jnp.swapaxes(rows_ref[pl.ds(0, len(rows)), :, COLS:], 0, 1)
        second_ref[...] = jnp.swapaxes(rows_ref[pl.ds(0, len(rows)), :, :COLS], 0, 1)


def conv(at, d, row_limit, own, halos, corners, weight, bias, hidden=None, runs=((0, ROWS),), carried=()):
    final = hidden is not None
    count = sum(n for _, n in runs)
    low, high = reach(runs)
    args = [at, d, row_limit, *own, *halos, weight, bias]
    in_specs = [SMEM] * 3 + [ANY] * 7 + [VMEM] * 2
    if needs_corners(runs):
        args += corners
        in_specs += [ANY] * 2
    if final:
        args += [hidden, *carried]
        in_specs += [ANY] + [VMEM] * len(carried)
    out_shape = [shape(C, count, COLS)] * 2 + [shape(C, LANES)] * 2 if final else [shape(ROWS, C, WIDE)] + EDGES
    scratch = [pltpu.VMEM((count, C, n), jnp.bfloat16) for n in ((WIDE, WIDE) if final else (WIDE, LANES, LANES))]
    return pl.pallas_call(
        functools.partial(conv_kernel, int(final), runs, len(carried)),
        in_specs=in_specs,
        out_specs=[VMEM if final else HBM] * len(out_shape),
        out_shape=out_shape,
        scratch_shapes=scratch
        + [pltpu.VMEM((high - low, C, n), jnp.bfloat16) for n in (WIDE, LANES, LANES, WIDE, WIDE)]
        + [pltpu.SemaphoreType.DMA((96,))],
        compiler_params=PARAMS,
        name="second" if final else "first",
    )(*args)


def behind_kernel(*refs):
    del refs


def behind(cells):
    return pl.pallas_call(
        behind_kernel,
        in_specs=[ANY] * len(cells),
        out_specs=[ANY] * len(cells),
        out_shape=[shape(*x.shape) for x in cells],
        input_output_aliases={i: i for i in range(len(cells))},
        compiler_params=PARAMS,
        name="behind",
    )(*cells)


def flat(weight):
    return jnp.transpose(weight, (1, 0, 2)).reshape(C, 9 * C)


def local(band_map, dilations, row_limit, weight_one, bias_one, weight_two, bias_two):
    at = whereabouts()
    vector = jnp.stack(at)
    early, late = routes(0), routes(1)

    own = [lax.ppermute(enter(i, vector, row_limit, band_map), AXES, routes(i)) for i in range(2)]
    weights = [flat(weight_one), flat(weight_two)]
    biases = [bias_one[:, None], bias_two[:, None]]
    halos, corners = exchange(at, *pack(vector, *own, weights + biases))
    hidden, *edges = conv(vector, dilations, row_limit, own, halos, corners, weights[0], biases[0])
    halos, corners = exchange(at, *edges)

    pos, off = lax.axis_index("pos"), lax.axis_index("off")
    here = lambda pairs: functools.reduce(jnp.logical_or, [(pos % 2 == s) & (off == b) for s, b in pairs])
    stays, relayed = here(STAY), here(VIA)
    kept = [(to, at_work) for to, at_work in late if (to // 8 % 2, to % 8) in STAY]
    lends = functools.reduce(jnp.logical_or, [(pos == a // 8) & (off == a % 8) for _, a in kept])

    def relay(pairs, turn):
        leave, arrive = [], []
        for to, at_work in pairs:
            stored, block = to // 8, to % 8
            if (stored % 2, block) in VIA:
                via = device(stored // 2, *VIA[stored % 2, block])
                leave.append((at_work, via))
                arrive.append((via, to))
            elif (stored % 2, block) not in STAY:
                leave.append((at_work, to))
            elif turn:
                arrive.append((at_work, to))
        return leave, arrive

    leave, arrive = relay(early, 0)
    leave_late, arrive_late = relay(late, 1)

    def second(rows, carried):
        return conv(
            vector, dilations, row_limit, own, halos, corners, weights[1], biases[1], hidden, rows, carried
        )

    def sorted_out(first, passed, ended):
        return jnp.where(stays, first, jnp.where(relayed, ended, passed))

    first, late_first, *carried = second(PARTS[0], [])
    passed = lax.ppermute(first, AXES, leave)
    through = lax.ppermute(late_first, AXES, leave_late)
    more, late_more, *carried = second(PARTS[1], carried)
    passed, through, more, late_more, edge, other = behind((passed, through, more, late_more, *carried))
    passed_more = lax.ppermute(more, AXES, leave)
    direct = lax.ppermute(late_more, AXES, [(b, a) for a, b in late])
    ended = lax.ppermute(passed, AXES, arrive)
    ended_late = lax.ppermute(jnp.where(lends, late_first, through), AXES, arrive_late)
    ended_more = lax.ppermute(passed_more, AXES, arrive)
    gots = [sorted_out(first, passed, ended), sorted_out(more, passed_more, ended_more)]
    directs = [jnp.where(stays | relayed, ended_late, through), direct]

    to_first = lambda core: [(place(s, f), home(s // 2, f + 1)) for s, f in CELLS if s % 2 == core]
    to_second = lambda core: [(place(s, f), home(s // 2, 8 - f)) for s, f in CELLS if s % 2 == core and f]
    edge = lax.ppermute(edge, AXES, to_first(0) + to_second(1))
    other = lax.ppermute(other, AXES, to_second(0) + to_first(1))
    low = at[STORED_BLOCK] <= 4
    halves = jnp.where(low, edge, other), jnp.where(low, other, edge)
    top_first = at[EARLY] == 0
    column = lax.broadcasted_iota(jnp.int32, (1, 1, COLS), 2)
    out = []
    for half in range(2):
        pieces = []
        for runs, *pair in zip(PARTS, gots, directs):
            got = jnp.where(top_first, *(pair if half == 0 else pair[::-1]))
            at_row = 0
            for start, count in runs:
                cells = lax.slice_in_dim(got, at_row, at_row + count, axis=1)
                edge = lax.slice_in_dim(halves[half], start, start + count, axis=1)[:, :, None]
                more = (cells.astype(jnp.float32) + 0.5 * edge.astype(jnp.float32)).astype(jnp.bfloat16)
                pieces.append((start, jnp.where(column == 0, more, cells)))
                at_row += count
        out += [piece for _, piece in sorted(pieces, key=lambda x: x[0])]
    return jnp.concatenate(out, axis=1)


def solution(mesh):
    in_specs = (P(None, "pos", "off"), P(), P(), P(), P(), P(), P())
    out_specs = P(None, "pos", "off")
    return jax.shard_map(local, mesh=mesh, in_specs=in_specs, out_specs=out_specs, check_vma=False)
```

```python
import functools

import jax
import jax.numpy as jnp
from jax import lax
from jax.experimental import pallas as pl
from jax.experimental.pallas import tpu as pltpu
from jax.sharding import PartitionSpec as P

BAND = 1024
DMAX = 32
C = 48
ROWS = 72
COLS = 256
WIDE = 2 * COLS
LANES = 128
HALO = DMAX
CORNER = DMAX // 2
CHUNK = 24
PARTS = (((0, 24),), ((24, 48),))
PREP = 8
UNROLL = 24
STACK = 8
AXES = ("pos", "off")

SMEM = pl.BlockSpec(memory_space=pltpu.SMEM)
VMEM = pl.BlockSpec(memory_space=pltpu.VMEM)
ANY = pl.BlockSpec(memory_space=pl.ANY)
HBM = pl.BlockSpec(memory_space=pltpu.HBM)
PARAMS = pltpu.CompilerParams(vmem_limit_bytes=63 * 2**20)


def device(pair, x, z, core):
    return (2 * pair + core) * 8 + 2 * z + x


def home(stored, block):
    return device(stored // 2, block % 2, block // 2, stored % 2)


def place(strip, fold):
    stored = strip // 2
    return device(stored // 2, stored % 2, (4 - fold) % 4, strip % 2)


def lead(stored, fold):
    return (fold == 1) & (stored % 2 == 0) | (fold == 3) & (stored % 2 == 1)


CELLS = [(strip, fold) for strip in range(32) for fold in range(4)]


def routes(turn):
    out = []
    for strip, fold in CELLS:
        core, stored = strip % 2, strip // 2
        first = (core == int(lead(stored, fold))) == (turn == 0)
        out.append((home(stored, fold if first else 7 - fold), place(strip, fold)))
    return out


VIA = {(0, 1): (0, 0, 0), (0, 7): (0, 3, 0), (1, 2): (1, 1, 1), (1, 4): (1, 2, 1)}
STAY = ((0, 0), (0, 6), (1, 3), (1, 5))


def whereabouts():
    pos, off = lax.axis_index("pos"), lax.axis_index("off")
    fold = jnp.minimum(off, 7 - off)
    early = jnp.where(off < 4, 0, 1) ^ lead(pos, fold).astype(jnp.int32)
    stored = 2 * (pos // 2) + off % 2
    core = pos % 2
    work = (4 - off // 2) % 4
    order = core ^ lead(stored, work).astype(jnp.int32)
    values = (pos * 2 * ROWS, off, early, stored * 2 * ROWS + core * ROWS, work, order, core)
    values += (jnp.where(work == 3, 2, work % 2), core + 2 * (work % 2))
    return [v.astype(jnp.int32) for v in values]


STORED_ROW, STORED_BLOCK, EARLY, ROW, FOLD, ORDER, CORE, SIDE, KIND = range(9)


def choose(at_ref, index, cases):
    for value, case in enumerate(cases):
        pl.when(at_ref[index] == value)(case)


def threshold(limit_ref, row):
    last = limit_ref.shape[0] - 1
    return jnp.minimum(limit_ref[row], jnp.minimum(2 * row + 1, 2 * last - 2 * row))


def offsets(block, dims):
    return jnp.abs(lax.broadcasted_iota(jnp.int32, dims, len(dims) - 1) + (block * COLS - BAND))


def both_offsets(fold):
    return jnp.concatenate([offsets(fold, (C, COLS)), offsets(7 - fold, (C, COLS))], axis=1)


def shape(*dims):
    return jax.ShapeDtypeStruct(dims, jnp.bfloat16)


def enter_kernel(turn, at_ref, limit_ref, x_ref, out_ref):
    x = jnp.swapaxes(x_ref[...], 0, 1)
    away = offsets(at_ref[STORED_BLOCK], (C, COLS))
    row0 = at_ref[STORED_ROW] + (at_ref[EARLY] ^ turn) * ROWS
    for i in range(ROWS):
        seen = away <= threshold(limit_ref, row0 + i)
        out_ref[i] = jnp.where(seen, x[i], jnp.zeros((), jnp.bfloat16))


def enter(turn, at, row_limit, band_map):
    return pl.pallas_call(
        functools.partial(enter_kernel, turn),
        grid_spec=pltpu.PrefetchScalarGridSpec(
            num_scalar_prefetch=1,
            grid=(1,),
            in_specs=[SMEM, pl.BlockSpec((C, ROWS, COLS), lambda i, at_ref: (0, at_ref[EARLY] ^ turn, 0))],
            out_specs=pl.BlockSpec((ROWS, C, COLS), lambda i, at_ref: (0, 0, 0)),
        ),
        out_shape=shape(ROWS, C, COLS),
        compiler_params=PARAMS,
        name="enter",
    )(at, row_limit, band_map)


EDGES = [shape(ROWS, C, LANES)] * 2 + [shape(HALO, C, WIDE)] * 2


def edge_copies(cells, first, count, top, bottom):
    out = []
    for target, at in ((top, 0), (bottom, ROWS - HALO)):
        low, high = max(first, at), min(first + count, at + HALO)
        if low < high:
            out.append((cells.at[pl.ds(low - first, high - low)], target.at[pl.ds(low - at, high - low)]))
    return out


def inward_outward(cells, lane):
    return (
        jnp.where(lane < 64, cells[:, 2 * LANES : 3 * LANES], cells[:, LANES : 2 * LANES]),
        jnp.where(lane < 64, cells[:, :LANES], cells[:, 3 * LANES :]),
    )


def pack_kernel(at_ref, early_ref, late_ref, *refs):
    near, far, mate, other, blocks, into, back, sems = refs[-8:]
    lane = lax.broadcasted_iota(jnp.int32, (C, LANES), 1)
    runs = [pl.ds(i, CHUNK) for i in range(0, ROWS, CHUNK)]

    def work(first, second, inward, outward, top, bottom):
        n = 0

        def copy(src, dst):
            nonlocal n
            n += 1
            made = pltpu.make_async_copy(src, dst, sems.at[n - 1])
            made.start()
            return made

        here = [[copy(x.at[run], blocks.at[i, run]) for i, x in enumerate((first, second))] for run in runs]
        sent = []
        for at, run, loads in zip(range(0, ROWS, CHUNK), runs, here):
            for load in loads:
                load.wait()
            for i in range(at, at + CHUNK):
                a, b = blocks[0, i], blocks[1, i]
                into[i] = jnp.where(lane < 64, b[:, :LANES], a[:, LANES:])
                back[i] = jnp.where(lane < 64, a[:, :LANES], b[:, LANES:])
            sent += [copy(into.at[run], inward.at[run]), copy(back.at[run], outward.at[run])]
            for i in range(2):
                lanes = pl.ds(i * COLS, COLS)
                for src, dst in edge_copies(blocks.at[i, run], at, CHUNK, top, bottom):
                    sent.append(copy(src, dst.at[:, :, lanes]))
        for done in sent:
            done.wait()

    for order in range(2):

        def case(kind):
            cells = (late_ref, early_ref) if order else (early_ref, late_ref)
            edges = (far, near) if kind // 2 else (near, far)
            rows = (mate, other) if kind % 2 else (other, mate)
            return lambda: work(*cells, *edges, *rows)

        @pl.when(at_ref[ORDER] == order)
        def _():
            choose(at_ref, KIND, [case(kind) for kind in range(4)])


def pack(at, early, late, after):
    return pl.pallas_call(
        pack_kernel,
        in_specs=[SMEM] + [ANY] * (2 + len(after)),
        out_specs=[HBM] * 4,
        out_shape=EDGES,
        scratch_shapes=[
            pltpu.VMEM((2, ROWS, C, COLS), jnp.bfloat16),
            pltpu.VMEM((ROWS, C, LANES), jnp.bfloat16),
            pltpu.VMEM((ROWS, C, LANES), jnp.bfloat16),
            pltpu.SemaphoreType.DMA((96,)),
        ],
        compiler_params=PARAMS,
        name="pack",
    )(at, early, late, *after)


MATES = [(place(s, f), place(s ^ 1, f)) for s, f in CELLS]
OTHERS = [(place(s, f), place(t, f)) for s, f in CELLS for t in [s + 1 if s % 2 else s - 1] if 0 <= t < 32]
NEAR = [(place(s, f), place(s, f ^ 1)) for s, f in CELLS]
FAR = [(place(s, f), place(s, 3 - f)) for s, f in CELLS if f in (1, 2)]


def exchange(at, near, far, mate, other):
    beside = far
    near = lax.ppermute(near, AXES, NEAR)
    far = lax.ppermute(far, AXES, FAR)
    mate = lax.ppermute(mate, AXES, MATES)
    other = lax.ppermute(other, AXES, OTHERS)
    lane = lax.broadcasted_iota(jnp.int32, (1, 1, LANES), 2)

    def ends(first):
        rows = lambda x: lax.dynamic_slice_in_dim(x, first, CORNER)
        packed = []
        for x in (rows(near), jnp.where(at[FOLD] == 3, rows(beside), rows(far))):
            turned = jnp.concatenate([x[CORNER // 2 :, :, 64:], x[CORNER // 2 :, :, :64]], axis=2)
            packed.append(jnp.where((lane < 32) | (lane >= 96), x[: CORNER // 2], turned))
        return jnp.concatenate(packed, axis=0)

    down = at[CORE] == 0
    corner_mate = lax.ppermute(ends(jnp.where(down, ROWS - CORNER, 0)), AXES, MATES)
    corner_other = lax.ppermute(ends(jnp.where(down, 0, ROWS - CORNER)), AXES, OTHERS)
    return (near, far, beside, mate, other), (corner_mate, corner_other)


def reach(runs):
    return runs[0][0] - HALO, sum(runs[-1]) + HALO


def needs_corners(runs):
    low, high = reach(runs)
    return low < CORNER - HALO or high > ROWS + HALO - CORNER


def conv_kernel(which, runs, extra, at_ref, d_ref, limit_ref, early_ref, late_ref, *refs):
    final = which == 1
    near, far, beside, mate, other, w_ref, b_ref = refs[:7]
    refs = refs[7:]
    if needs_corners(runs):
        (corner_mate, corner_other), refs = refs[:2], refs[2:]
    if final:
        hidden_ref, carried, refs = refs[0], refs[1 : 1 + extra], refs[1 + extra :]
        outs, scratch = refs[:4], refs[4:]
        out_ref, own, mid, before, behind, plus_ref, minus_ref, packed_ref, sems = scratch
    else:
        outs, scratch = refs[:5], refs[5:]
        out_ref, in_ref, back_ref, mid, before, behind, plus_ref, minus_ref, packed_ref, sems = scratch

    base, end = reach(runs)
    made = []

    def copy(src, dst):
        made.append(pltpu.make_async_copy(src, dst, sems.at[len(made)]))
        return made[-1]

    def fetch(src, low, high, target, shift):
        low, high = max(low, base), min(high, end)
        if low >= high:
            return []
        return [copy(src.at[pl.ds(low - shift, high - low)], target.at[pl.ds(low - base, high - low)])]

    def own_cells(low, count, target, at):
        rows, to = pl.ds(low, count), pl.ds(at, count)
        lanes = [pl.ds(i * COLS, COLS) for i in range(2)]
        return [
            [copy(x.at[rows], target.at[to, :, lane]) for x, lane in zip(pair, lanes)]
            for pair in ((early_ref, late_ref), (late_ref, early_ref))
        ]

    def each(choice, act):
        index, groups = choice

        def case(group):
            return lambda: [act(c) for c in group] and None

        choose(at_ref, index, [case(group) for group in groups])

    rows = [
        fetch(above, -HALO, 0, mid, -HALO) + fetch(below, ROWS, ROWS + HALO, mid, ROWS)
        for above, below in ((other, mate), (mate, other))
    ]
    sides = [
        fetch(near, 0, ROWS, a, 0) + fetch(x, 0, ROWS, b, 0)
        for a, b, x in ((behind, before, far), (before, behind, far), (before, behind, beside))
    ]
    choices = [(CORE, rows), (SIDE, sides)]
    always = []
    later = []
    if needs_corners(runs):
        always += [copy(corner_mate, packed_ref.at[0]), copy(corner_other, packed_ref.at[1])]
    if final:
        always += fetch(hidden_ref, 0, ROWS, mid, 0)
        at = 0
        for first, count in runs:
            later.append((ORDER, own_cells(first, count, own, at)))
            at += count
    else:
        low, high = max(base, 0), min(end, ROWS)
        choices.append((ORDER, own_cells(low, high - low, mid, low - base)))
    for c in always:
        c.start()
    for choice in choices + later:
        each(choice, lambda c: c.start())
    for c in always:
        c.wait()
    for choice in choices:
        each(choice, lambda c: c.wait())

    def corners(kind):
        above, below = (0, 1) if kind % 2 else (1, 0)
        sides = (before, behind) if kind // 2 else (behind, before)

        def case():
            for which, low in ((above, -CORNER), (below, ROWS)):
                if low < base or low + CORNER > end:
                    continue
                for i, side in enumerate(sides):
                    for j in range(CORNER // 2):
                        cells = packed_ref[which, i * CORNER // 2 + j]
                        side[low - base + j] = cells
                        side[low - base + CORNER // 2 + j] = pltpu.roll(cells, 64, axis=1)

        return case

    if needs_corners(runs):
        choose(at_ref, KIND, [corners(kind) for kind in range(4)])

    d = d_ref[which]
    lo = d // 2
    hi = (d + 1) // 2
    odd = d - 2 * lo
    lane = lax.broadcasted_iota(jnp.int32, (C, LANES), 1)
    even_lane = (lane & 1) == 0

    def tiles(r):
        own = [mid[r, :, LANES * i : LANES * (i + 1)] for i in range(4)]
        return [before[r], *own[:2], behind[r], *own[2:]]

    def shifted(t, step, back):
        keep = lane < (step if back else LANES - step)
        turn = step if back else LANES - step
        left, a, b, right, c, e = t
        runs = ((left, a, b), (right, c, e)) if back else ((a, b, right), (c, e, left))
        out = []
        for run in runs:
            x, y, z = [pltpu.roll(v, turn, axis=1) for v in run]
            out += [jnp.where(keep, x, y), jnp.where(keep, y, z)]
        return jnp.concatenate(out, axis=1)

    for first, count in runs:
        start = first - base - hi

        def prepare(i, _):
            for j in range(PREP):
                r = start + i * PREP + j
                x, y = tiles(r), tiles(r + odd)
                both = [jnp.where(even_lane, b, a) for a, b in zip(x, y)]
                plus_ref[r] = shifted(both, d, False)
                minus_ref[r] = shifted(both, d, True)
            return 0

        lax.fori_loop(0, (count + d + PREP - 1) // PREP, prepare, 0)

    for choice in later:
        each(choice, lambda c: c.wait())
    weight = w_ref[...]
    bias = b_ref[...]
    away = both_offsets(at_ref[FOLD])
    row0 = at_ref[ROW]

    def row(ahead, m, _):
        r = m + ahead - base
        x = tiles(r)
        taps = [
            mid[r - d],
            plus_ref[r - hi],
            shifted(x, 2 * d, False),
            minus_ref[r - hi],
            mid[r],
            plus_ref[r + lo],
            shifted(x, 2 * d, True),
            minus_ref[r + lo],
            mid[r + d],
        ]
        acc = lax.dot_general(
            weight,
            jnp.concatenate(taps, axis=0),
            (((1,), (0,)), ((), ())),
            preferred_element_type=jnp.float32,
        )
        acc = acc + bias
        if final:
            acc = acc + own[m].astype(jnp.float32)
        else:
            acc = jnp.maximum(acc, 0.0)
        acc = jnp.where(away <= threshold(limit_ref, row0 + ahead + m), acc, 0.0).astype(jnp.bfloat16)
        out_ref[m] = acc
        if not final:
            in_ref[m], back_ref[m] = inward_outward(acc, lane)
        return 0

    if final:
        at = 0
        for first, count in runs:
            lax.fori_loop(at, at + count, functools.partial(row, first - at), 0, unroll=UNROLL)
            at += count
        mix(at_ref, limit_ref, runs, out_ref, carried, *outs, plus_ref)
        return
    hidden, to_near, to_far, to_mate, to_other = outs
    copies, ways = [], [[] for _ in range(4)]
    for at in range(0, ROWS, CHUNK):
        lax.fori_loop(at, at + CHUNK, functools.partial(row, 0), 0, unroll=UNROLL)
        run = pl.ds(at, CHUNK)
        copies.append(copy(out_ref.at[run], hidden.at[run]))
        copies[-1].start()
        more = []
        for kind in range(4):
            top, bottom = (to_mate, to_other) if kind % 2 else (to_other, to_mate)
            inward, outward = (to_far, to_near) if kind // 2 else (to_near, to_far)
            pairs = [(in_ref.at[run], inward.at[run]), (back_ref.at[run], outward.at[run])]
            pairs += edge_copies(out_ref.at[run], at, CHUNK, top, bottom)
            more.append([copy(a, b) for a, b in pairs])
        each((KIND, more), lambda c: c.start())
        for way, group in zip(ways, more):
            way += group
    for c in copies:
        c.wait()
    each((KIND, ways), lambda c: c.wait())


def mix(at_ref, limit_ref, runs, summed, carried, first_ref, second_ref, edge_ref, other_ref, rows_ref):
    a = lax.broadcasted_iota(jnp.int32, (COLS, COLS), 0)
    b = lax.broadcasted_iota(jnp.int32, (COLS, COLS), 1)
    turn = (a + b == COLS).astype(jnp.bfloat16)
    lane = lax.broadcasted_iota(jnp.int32, (C, LANES), 1)
    away = both_offsets(at_ref[FOLD])
    row0 = at_ref[ROW]
    rows = [first + i for first, count in runs for i in range(count)]
    swap = at_ref[CORE] == 0
    edges = [jnp.zeros((C, LANES), jnp.bfloat16)] * 2
    if carried:
        edge, other = carried[0][...], carried[1][...]
        edges = [jnp.where(swap, other, edge), jnp.where(swap, edge, other)]
    for group in range(len(rows) // STACK):
        at = group * STACK
        cells = summed[pl.ds(at, STACK)].reshape(STACK * C, WIDE)
        blocks = cells[:, :COLS], cells[:, COLS:]
        turned = [jnp.dot(x, turn, preferred_element_type=jnp.float32) for x in blocks]
        for i in range(2):
            mean = 0.5 * (blocks[i].astype(jnp.float32) + turned[1 - i])
            for j in range(STACK):
                m = at + j
                part = slice(C * j, C * (j + 1))
                seen = away[:, COLS * i : COLS * (i + 1)] <= threshold(limit_ref, row0 + rows[m])
                rows_ref[m, :, COLS * i : COLS * (i + 1)] = jnp.where(seen, mean[part], 0.0).astype(jnp.bfloat16)
                tile = blocks[i][part, :LANES]
                tile = pltpu.roll(tile, rows[m], axis=1) if rows[m] else tile
                edges[i] = jnp.where(lane == rows[m], tile, edges[i])
    edge_ref[...] = jnp.where(swap, edges[1], edges[0])
    other_ref[...] = jnp.where(swap, edges[0], edges[1])
    early = at_ref[ORDER] == 0

    @pl.when(early)
    def _():
        first_ref[...] = jnp.swapaxes(rows_ref[pl.ds(0, len(rows)), :, :COLS], 0, 1)
        second_ref[...] = jnp.swapaxes(rows_ref[pl.ds(0, len(rows)), :, COLS:], 0, 1)

    @pl.when(jnp.logical_not(early))
    def _():
        first_ref[...] = jnp.swapaxes(rows_ref[pl.ds(0, len(rows)), :, COLS:], 0, 1)
        second_ref[...] = jnp.swapaxes(rows_ref[pl.ds(0, len(rows)), :, :COLS], 0, 1)


def conv(at, d, row_limit, own, halos, corners, weight, bias, hidden=None, runs=((0, ROWS),), carried=()):
    final = hidden is not None
    count = sum(n for _, n in runs)
    low, high = reach(runs)
    args = [at, d, row_limit, *own, *halos, weight, bias]
    in_specs = [SMEM] * 3 + [ANY] * 7 + [VMEM] * 2
    if needs_corners(runs):
        args += corners
        in_specs += [HBM] * 2
    if final:
        args += [hidden, *carried]
        in_specs += [ANY] + [VMEM] * len(carried)
    out_shape = [shape(C, count, COLS)] * 2 + [shape(C, LANES)] * 2 if final else [shape(ROWS, C, WIDE)] + EDGES
    scratch = [pltpu.VMEM((count, C, n), jnp.bfloat16) for n in ((WIDE, WIDE) if final else (WIDE, LANES, LANES))]
    return pl.pallas_call(
        functools.partial(conv_kernel, int(final), runs, len(carried)),
        in_specs=in_specs,
        out_specs=[VMEM if final else HBM] * len(out_shape),
        out_shape=out_shape,
        scratch_shapes=scratch
        + [pltpu.VMEM((high - low, C, n), jnp.bfloat16) for n in (WIDE, LANES, LANES, WIDE, WIDE)]
        + [pltpu.VMEM((2, CORNER, C, LANES), jnp.bfloat16)]
        + [pltpu.SemaphoreType.DMA((96,))],
        compiler_params=PARAMS,
        name="second" if final else "first",
    )(*args)


def behind_kernel(*refs):
    del refs


def behind(cells):
    return pl.pallas_call(
        behind_kernel,
        in_specs=[HBM] * len(cells),
        out_specs=[HBM] * len(cells),
        out_shape=[shape(*x.shape) for x in cells],
        input_output_aliases={i: i for i in range(len(cells))},
        compiler_params=PARAMS,
        name="behind",
    )(*cells)


def flat(weight):
    return jnp.transpose(weight, (1, 0, 2)).reshape(C, 9 * C)


def local(band_map, dilations, row_limit, weight_one, bias_one, weight_two, bias_two):
    at = whereabouts()
    vector = jnp.stack(at)
    early, late = routes(0), routes(1)

    own = [lax.ppermute(enter(i, vector, row_limit, band_map), AXES, routes(i)) for i in range(2)]
    weights = [flat(weight_one), flat(weight_two)]
    biases = [bias_one[:, None], bias_two[:, None]]
    halos, corners = exchange(at, *pack(vector, *own, weights + biases))
    hidden, *edges = conv(vector, dilations, row_limit, own, halos, corners, weights[0], biases[0])
    halos, corners = exchange(at, *edges)

    pos, off = lax.axis_index("pos"), lax.axis_index("off")
    here = lambda pairs: functools.reduce(jnp.logical_or, [(pos % 2 == s) & (off == b) for s, b in pairs])
    stays, relayed = here(STAY), here(VIA)
    leave, arrive = [], []
    for to, at_work in early:
        stored, block = to // 8, to % 8
        if (stored % 2, block) in VIA:
            via = device(stored // 2, *VIA[stored % 2, block])
            leave.append((at_work, via))
            arrive.append((via, to))
        elif at_work != to:
            leave.append((at_work, to))

    def second(rows, carried):
        return conv(
            vector, dilations, row_limit, own, halos, corners, weights[1], biases[1], hidden, rows, carried
        )

    def sorted_out(first, passed, ended):
        return jnp.where(stays, first, jnp.where(relayed, ended, passed))

    straight = [(b, a) for a, b in late]
    first, late_first, *carried = second(PARTS[0], [])
    passed = lax.ppermute(first, AXES, leave)
    direct = lax.ppermute(late_first, AXES, straight)
    more, late_more, *carried = second(PARTS[1], carried)
    passed, direct, more, late_more, edge, other = behind((passed, direct, more, late_more, *carried))
    passed_more = lax.ppermute(more, AXES, leave)
    direct_more = lax.ppermute(late_more, AXES, straight)
    ended = lax.ppermute(passed, AXES, arrive)
    ended_more = lax.ppermute(passed_more, AXES, arrive)
    gots = [sorted_out(first, passed, ended), sorted_out(more, passed_more, ended_more)]
    directs = [direct, direct_more]

    to_first = lambda core: [(place(s, f), home(s // 2, f + 1)) for s, f in CELLS if s % 2 == core]
    to_second = lambda core: [(place(s, f), home(s // 2, 8 - f)) for s, f in CELLS if s % 2 == core and f]
    edge = lax.ppermute(edge, AXES, to_first(0) + to_second(1))
    other = lax.ppermute(other, AXES, to_second(0) + to_first(1))
    low = at[STORED_BLOCK] <= 4
    halves = jnp.where(low, edge, other), jnp.where(low, other, edge)
    top_first = at[EARLY] == 0
    column = lax.broadcasted_iota(jnp.int32, (1, 1, COLS), 2)
    out = []
    for half in range(2):
        pieces = []
        for runs, *pair in zip(PARTS, gots, directs):
            got = jnp.where(top_first, *(pair if half == 0 else pair[::-1]))
            at_row = 0
            for start, count in runs:
                cells = lax.slice_in_dim(got, at_row, at_row + count, axis=1)
                edge = lax.slice_in_dim(halves[half], start, start + count, axis=1)[:, :, None]
                more = (cells.astype(jnp.float32) + 0.5 * edge.astype(jnp.float32)).astype(jnp.bfloat16)
                pieces.append((start, jnp.where(column == 0, more, cells)))
                at_row += count
        out += [piece for _, piece in sorted(pieces, key=lambda x: x[0])]
    return jnp.concatenate(out, axis=1)


def solution(mesh):
    in_specs = (P(None, "pos", "off"), P(), P(), P(), P(), P(), P())
    out_specs = P(None, "pos", "off")
    return jax.shard_map(local, mesh=mesh, in_specs=in_specs, out_specs=out_specs, check_vma=False)
```

```python
import functools

import jax
import jax.numpy as jnp
from jax import lax
from jax.experimental import pallas as pl
from jax.experimental.pallas import tpu as pltpu
from jax.sharding import PartitionSpec as P

BAND = 1024
DMAX = 32
C = 48
ROWS = 72
COLS = 256
WIDE = 2 * COLS
LANES = 128
HALO = DMAX
CORNER = DMAX // 2
CHUNK = 24
PARTS = (((0, 24),), ((24, 48),))
PREP = 8
UNROLL = 24
STACK = 12
AXES = ("pos", "off")

SMEM = pl.BlockSpec(memory_space=pltpu.SMEM)
VMEM = pl.BlockSpec(memory_space=pltpu.VMEM)
ANY = pl.BlockSpec(memory_space=pl.ANY)
HBM = pl.BlockSpec(memory_space=pltpu.HBM)
PARAMS = pltpu.CompilerParams(vmem_limit_bytes=63 * 2**20)


def device(pair, x, z, core):
    return (2 * pair + core) * 8 + 2 * z + x


def home(stored, block):
    return device(stored // 2, block % 2, block // 2, stored % 2)


def place(strip, fold):
    stored = strip // 2
    return device(stored // 2, stored % 2, (4 - fold) % 4, strip % 2)


def lead(stored, fold):
    return (fold == 1) & (stored % 2 == 0) | (fold == 3) & (stored % 2 == 1)


CELLS = [(strip, fold) for strip in range(32) for fold in range(4)]


def routes(turn):
    out = []
    for strip, fold in CELLS:
        core, stored = strip % 2, strip // 2
        first = (core == int(lead(stored, fold))) == (turn == 0)
        out.append((home(stored, fold if first else 7 - fold), place(strip, fold)))
    return out


VIA = {(0, 1): (0, 0, 0), (0, 7): (0, 3, 0), (1, 2): (1, 1, 1), (1, 4): (1, 2, 1)}
STAY = ((0, 0), (0, 6), (1, 3), (1, 5))


def whereabouts():
    pos, off = lax.axis_index("pos"), lax.axis_index("off")
    fold = jnp.minimum(off, 7 - off)
    early = jnp.where(off < 4, 0, 1) ^ lead(pos, fold).astype(jnp.int32)
    stored = 2 * (pos // 2) + off % 2
    core = pos % 2
    work = (4 - off // 2) % 4
    order = core ^ lead(stored, work).astype(jnp.int32)
    values = (pos * 2 * ROWS, off, early, stored * 2 * ROWS + core * ROWS, work, order, core)
    values += (jnp.where(work == 3, 2, work % 2), core + 2 * (work % 2))
    return [v.astype(jnp.int32) for v in values]


STORED_ROW, STORED_BLOCK, EARLY, ROW, FOLD, ORDER, CORE, SIDE, KIND = range(9)


def choose(at_ref, index, cases):
    for value, case in enumerate(cases):
        pl.when(at_ref[index] == value)(case)


def threshold(limit_ref, row):
    last = limit_ref.shape[0] - 1
    return jnp.minimum(limit_ref[row], jnp.minimum(2 * row + 1, 2 * last - 2 * row))


def offsets(block, dims):
    return jnp.abs(lax.broadcasted_iota(jnp.int32, dims, len(dims) - 1) + (block * COLS - BAND))


def both_offsets(fold):
    return jnp.concatenate([offsets(fold, (C, COLS)), offsets(7 - fold, (C, COLS))], axis=1)


def shape(*dims):
    return jax.ShapeDtypeStruct(dims, jnp.bfloat16)


def enter_kernel(turn, at_ref, limit_ref, x_ref, out_ref):
    x = jnp.swapaxes(x_ref[...], 0, 1)
    away = offsets(at_ref[STORED_BLOCK], (C, COLS))
    row0 = at_ref[STORED_ROW] + (at_ref[EARLY] ^ turn) * ROWS
    for i in range(ROWS):
        seen = away <= threshold(limit_ref, row0 + i)
        out_ref[i] = jnp.where(seen, x[i], jnp.zeros((), jnp.bfloat16))


def enter(turn, at, row_limit, band_map):
    return pl.pallas_call(
        functools.partial(enter_kernel, turn),
        grid_spec=pltpu.PrefetchScalarGridSpec(
            num_scalar_prefetch=1,
            grid=(1,),
            in_specs=[SMEM, pl.BlockSpec((C, ROWS, COLS), lambda i, at_ref: (0, at_ref[EARLY] ^ turn, 0))],
            out_specs=pl.BlockSpec((ROWS, C, COLS), lambda i, at_ref: (0, 0, 0)),
        ),
        out_shape=shape(ROWS, C, COLS),
        compiler_params=PARAMS,
        name="enter",
    )(at, row_limit, band_map)


EDGES = [shape(ROWS, C, LANES)] * 2 + [shape(HALO, C, WIDE)] * 2


def edge_copies(cells, first, count, top, bottom):
    out = []
    for target, at in ((top, 0), (bottom, ROWS - HALO)):
        low, high = max(first, at), min(first + count, at + HALO)
        if low < high:
            out.append((cells.at[pl.ds(low - first, high - low)], target.at[pl.ds(low - at, high - low)]))
    return out


def inward_outward(cells, lane):
    return (
        jnp.where(lane < 64, cells[:, 2 * LANES : 3 * LANES], cells[:, LANES : 2 * LANES]),
        jnp.where(lane < 64, cells[:, :LANES], cells[:, 3 * LANES :]),
    )


def pack_kernel(at_ref, early_ref, late_ref, *refs):
    near, far, mate, other, blocks, into, back, sems = refs[-8:]
    lane = lax.broadcasted_iota(jnp.int32, (C, LANES), 1)
    runs = [pl.ds(i, CHUNK) for i in range(0, ROWS, CHUNK)]

    def work(first, second, inward, outward, top, bottom):
        n = 0

        def copy(src, dst):
            nonlocal n
            n += 1
            made = pltpu.make_async_copy(src, dst, sems.at[n - 1])
            made.start()
            return made

        here = [[copy(x.at[run], blocks.at[i, run]) for i, x in enumerate((first, second))] for run in runs]
        sent = []
        for at, run, loads in zip(range(0, ROWS, CHUNK), runs, here):
            for load in loads:
                load.wait()
            for i in range(at, at + CHUNK):
                a, b = blocks[0, i], blocks[1, i]
                into[i] = jnp.where(lane < 64, b[:, :LANES], a[:, LANES:])
                back[i] = jnp.where(lane < 64, a[:, :LANES], b[:, LANES:])
            sent += [copy(into.at[run], inward.at[run]), copy(back.at[run], outward.at[run])]
            for i in range(2):
                lanes = pl.ds(i * COLS, COLS)
                for src, dst in edge_copies(blocks.at[i, run], at, CHUNK, top, bottom):
                    sent.append(copy(src, dst.at[:, :, lanes]))
        for done in sent:
            done.wait()

    for order in range(2):

        def case(kind):
            cells = (late_ref, early_ref) if order else (early_ref, late_ref)
            edges = (far, near) if kind // 2 else (near, far)
            rows = (mate, other) if kind % 2 else (other, mate)
            return lambda: work(*cells, *edges, *rows)

        @pl.when(at_ref[ORDER] == order)
        def _():
            choose(at_ref, KIND, [case(kind) for kind in range(4)])


def pack(at, early, late, after):
    return pl.pallas_call(
        pack_kernel,
        in_specs=[SMEM] + [ANY] * (2 + len(after)),
        out_specs=[HBM] * 4,
        out_shape=EDGES,
        scratch_shapes=[
            pltpu.VMEM((2, ROWS, C, COLS), jnp.bfloat16),
            pltpu.VMEM((ROWS, C, LANES), jnp.bfloat16),
            pltpu.VMEM((ROWS, C, LANES), jnp.bfloat16),
            pltpu.SemaphoreType.DMA((96,)),
        ],
        compiler_params=PARAMS,
        name="pack",
    )(at, early, late, *after)


MATES = [(place(s, f), place(s ^ 1, f)) for s, f in CELLS]
OTHERS = [(place(s, f), place(t, f)) for s, f in CELLS for t in [s + 1 if s % 2 else s - 1] if 0 <= t < 32]
NEAR = [(place(s, f), place(s, f ^ 1)) for s, f in CELLS]
FAR = [(place(s, f), place(s, 3 - f)) for s, f in CELLS if f in (1, 2)]


def exchange(at, near, far, mate, other):
    beside = far
    near = lax.ppermute(near, AXES, NEAR)
    far = lax.ppermute(far, AXES, FAR)
    mate = lax.ppermute(mate, AXES, MATES)
    other = lax.ppermute(other, AXES, OTHERS)
    lane = lax.broadcasted_iota(jnp.int32, (1, 1, LANES), 2)

    def ends(first):
        rows = lambda x: lax.dynamic_slice_in_dim(x, first, CORNER)
        packed = []
        for x in (rows(near), jnp.where(at[FOLD] == 3, rows(beside), rows(far))):
            turned = jnp.concatenate([x[CORNER // 2 :, :, 64:], x[CORNER // 2 :, :, :64]], axis=2)
            packed.append(jnp.where((lane < 32) | (lane >= 96), x[: CORNER // 2], turned))
        return jnp.concatenate(packed, axis=0)

    down = at[CORE] == 0
    corner_mate = lax.ppermute(ends(jnp.where(down, ROWS - CORNER, 0)), AXES, MATES)
    corner_other = lax.ppermute(ends(jnp.where(down, 0, ROWS - CORNER)), AXES, OTHERS)
    return (near, far, beside, mate, other), (corner_mate, corner_other)


def reach(runs):
    return runs[0][0] - HALO, sum(runs[-1]) + HALO


def needs_corners(runs):
    low, high = reach(runs)
    return low < CORNER - HALO or high > ROWS + HALO - CORNER


def conv_kernel(which, runs, extra, at_ref, d_ref, limit_ref, early_ref, late_ref, *refs):
    final = which == 1
    near, far, beside, mate, other, w_ref, b_ref = refs[:7]
    refs = refs[7:]
    if needs_corners(runs):
        (corner_mate, corner_other), refs = refs[:2], refs[2:]
    if final:
        hidden_ref, carried, refs = refs[0], refs[1 : 1 + extra], refs[1 + extra :]
        outs, scratch = refs[:4], refs[4:]
        out_ref, own, mid, before, behind, plus_ref, minus_ref, packed_ref, sems = scratch
    else:
        outs, scratch = refs[:5], refs[5:]
        out_ref, in_ref, back_ref, mid, before, behind, plus_ref, minus_ref, packed_ref, sems = scratch

    base, end = reach(runs)
    made = []

    def copy(src, dst):
        made.append(pltpu.make_async_copy(src, dst, sems.at[len(made)]))
        return made[-1]

    def fetch(src, low, high, target, shift):
        low, high = max(low, base), min(high, end)
        if low >= high:
            return []
        return [copy(src.at[pl.ds(low - shift, high - low)], target.at[pl.ds(low - base, high - low)])]

    def own_cells(low, count, target, at):
        rows, to = pl.ds(low, count), pl.ds(at, count)
        lanes = [pl.ds(i * COLS, COLS) for i in range(2)]
        return [
            [copy(x.at[rows], target.at[to, :, lane]) for x, lane in zip(pair, lanes)]
            for pair in ((early_ref, late_ref), (late_ref, early_ref))
        ]

    def each(choice, act):
        index, groups = choice

        def case(group):
            return lambda: [act(c) for c in group] and None

        choose(at_ref, index, [case(group) for group in groups])

    rows = [
        fetch(above, -HALO, 0, mid, -HALO) + fetch(below, ROWS, ROWS + HALO, mid, ROWS)
        for above, below in ((other, mate), (mate, other))
    ]
    sides = [
        fetch(near, 0, ROWS, a, 0) + fetch(x, 0, ROWS, b, 0)
        for a, b, x in ((behind, before, far), (before, behind, far), (before, behind, beside))
    ]
    choices = [(CORE, rows), (SIDE, sides)]
    always = []
    later = []
    if needs_corners(runs):
        always += [copy(corner_mate, packed_ref.at[0]), copy(corner_other, packed_ref.at[1])]
    if final:
        always += fetch(hidden_ref, 0, ROWS, mid, 0)
        at = 0
        for first, count in runs:
            later.append((ORDER, own_cells(first, count, own, at)))
            at += count
    else:
        low, high = max(base, 0), min(end, ROWS)
        choices.append((ORDER, own_cells(low, high - low, mid, low - base)))
    for c in always:
        c.start()
    for choice in choices + later:
        each(choice, lambda c: c.start())
    for c in always:
        c.wait()
    for choice in choices:
        each(choice, lambda c: c.wait())

    def corners(kind):
        above, below = (0, 1) if kind % 2 else (1, 0)
        sides = (before, behind) if kind // 2 else (behind, before)

        def case():
            for which, low in ((above, -CORNER), (below, ROWS)):
                if low < base or low + CORNER > end:
                    continue
                for i, side in enumerate(sides):
                    for j in range(CORNER // 2):
                        cells = packed_ref[which, i * CORNER // 2 + j]
                        side[low - base + j] = cells
                        side[low - base + CORNER // 2 + j] = pltpu.roll(cells, 64, axis=1)

        return case

    if needs_corners(runs):
        choose(at_ref, KIND, [corners(kind) for kind in range(4)])

    d = d_ref[which]
    lo = d // 2
    hi = (d + 1) // 2
    odd = d - 2 * lo
    lane = lax.broadcasted_iota(jnp.int32, (C, LANES), 1)
    even_lane = (lane & 1) == 0

    def tiles(r):
        own = [mid[r, :, LANES * i : LANES * (i + 1)] for i in range(4)]
        return [before[r], *own[:2], behind[r], *own[2:]]

    def shifted(t, step, back):
        keep = lane < (step if back else LANES - step)
        turn = step if back else LANES - step
        left, a, b, right, c, e = t
        runs = ((left, a, b), (right, c, e)) if back else ((a, b, right), (c, e, left))
        out = []
        for run in runs:
            x, y, z = [pltpu.roll(v, turn, axis=1) for v in run]
            out += [jnp.where(keep, x, y), jnp.where(keep, y, z)]
        return jnp.concatenate(out, axis=1)

    for first, count in runs:
        start = first - base - hi

        def prepare(i, _):
            for j in range(PREP):
                r = start + i * PREP + j
                x, y = tiles(r), tiles(r + odd)
                both = [jnp.where(even_lane, b, a) for a, b in zip(x, y)]
                plus_ref[r] = shifted(both, d, False)
                minus_ref[r] = shifted(both, d, True)
            return 0

        lax.fori_loop(0, (count + d + PREP - 1) // PREP, prepare, 0)

    for choice in later:
        each(choice, lambda c: c.wait())
    weight = w_ref[...]
    bias = b_ref[...]
    away = both_offsets(at_ref[FOLD])
    row0 = at_ref[ROW]

    def row(ahead, m, _):
        r = m + ahead - base
        x = tiles(r)
        taps = [
            mid[r - d],
            plus_ref[r - hi],
            shifted(x, 2 * d, False),
            minus_ref[r - hi],
            mid[r],
            plus_ref[r + lo],
            shifted(x, 2 * d, True),
            minus_ref[r + lo],
            mid[r + d],
        ]
        acc = lax.dot_general(
            weight,
            jnp.concatenate(taps, axis=0),
            (((1,), (0,)), ((), ())),
            preferred_element_type=jnp.float32,
        )
        acc = acc + bias
        if final:
            acc = acc + own[m].astype(jnp.float32)
        else:
            acc = jnp.maximum(acc, 0.0)
        acc = jnp.where(away <= threshold(limit_ref, row0 + ahead + m), acc, 0.0).astype(jnp.bfloat16)
        out_ref[m] = acc
        if not final:
            in_ref[m], back_ref[m] = inward_outward(acc, lane)
        return 0

    if final:
        at = 0
        for first, count in runs:
            lax.fori_loop(at, at + count, functools.partial(row, first - at), 0, unroll=UNROLL)
            at += count
        mix(at_ref, limit_ref, runs, out_ref, carried, *outs, plus_ref)
        return
    hidden, to_near, to_far, to_mate, to_other = outs
    copies, ways = [], [[] for _ in range(4)]
    for at in range(0, ROWS, CHUNK):
        lax.fori_loop(at, at + CHUNK, functools.partial(row, 0), 0, unroll=UNROLL)
        run = pl.ds(at, CHUNK)
        copies.append(copy(out_ref.at[run], hidden.at[run]))
        copies[-1].start()
        more = []
        for kind in range(4):
            top, bottom = (to_mate, to_other) if kind % 2 else (to_other, to_mate)
            inward, outward = (to_far, to_near) if kind // 2 else (to_near, to_far)
            pairs = [(in_ref.at[run], inward.at[run]), (back_ref.at[run], outward.at[run])]
            pairs += edge_copies(out_ref.at[run], at, CHUNK, top, bottom)
            more.append([copy(a, b) for a, b in pairs])
        each((KIND, more), lambda c: c.start())
        for way, group in zip(ways, more):
            way += group
    for c in copies:
        c.wait()
    each((KIND, ways), lambda c: c.wait())


def mix(at_ref, limit_ref, runs, summed, carried, first_ref, second_ref, edge_ref, other_ref, rows_ref):
    a = lax.broadcasted_iota(jnp.int32, (COLS, COLS), 0)
    b = lax.broadcasted_iota(jnp.int32, (COLS, COLS), 1)
    turn = (a + b == COLS).astype(jnp.bfloat16)
    lane = lax.broadcasted_iota(jnp.int32, (C, LANES), 1)
    away = both_offsets(at_ref[FOLD])
    row0 = at_ref[ROW]
    rows = [first + i for first, count in runs for i in range(count)]
    swap = at_ref[CORE] == 0
    edges = [jnp.zeros((C, LANES), jnp.bfloat16)] * 2
    if carried:
        edge, other = carried[0][...], carried[1][...]
        edges = [jnp.where(swap, other, edge), jnp.where(swap, edge, other)]
    for group in range(len(rows) // STACK):
        at = group * STACK
        cells = summed[pl.ds(at, STACK)].reshape(STACK * C, WIDE)
        blocks = cells[:, :COLS], cells[:, COLS:]
        turned = [jnp.dot(x, turn, preferred_element_type=jnp.float32) for x in blocks]
        for i in range(2):
            mean = 0.5 * (blocks[i].astype(jnp.float32) + turned[1 - i])
            for j in range(STACK):
                m = at + j
                part = slice(C * j, C * (j + 1))
                seen = away[:, COLS * i : COLS * (i + 1)] <= threshold(limit_ref, row0 + rows[m])
                rows_ref[m, :, COLS * i : COLS * (i + 1)] = jnp.where(seen, mean[part], 0.0).astype(jnp.bfloat16)
                tile = blocks[i][part, :LANES]
                tile = pltpu.roll(tile, rows[m], axis=1) if rows[m] else tile
                edges[i] = jnp.where(lane == rows[m], tile, edges[i])
    edge_ref[...] = jnp.where(swap, edges[1], edges[0])
    other_ref[...] = jnp.where(swap, edges[0], edges[1])
    early = at_ref[ORDER] == 0

    @pl.when(early)
    def _():
        first_ref[...] = jnp.swapaxes(rows_ref[pl.ds(0, len(rows)), :, :COLS], 0, 1)
        second_ref[...] = jnp.swapaxes(rows_ref[pl.ds(0, len(rows)), :, COLS:], 0, 1)

    @pl.when(jnp.logical_not(early))
    def _():
        first_ref[...] = jnp.swapaxes(rows_ref[pl.ds(0, len(rows)), :, COLS:], 0, 1)
        second_ref[...] = jnp.swapaxes(rows_ref[pl.ds(0, len(rows)), :, :COLS], 0, 1)


def conv(at, d, row_limit, own, halos, corners, weight, bias, hidden=None, runs=((0, ROWS),), carried=()):
    final = hidden is not None
    count = sum(n for _, n in runs)
    low, high = reach(runs)
    args = [at, d, row_limit, *own, *halos, weight, bias]
    in_specs = [SMEM] * 3 + [ANY] * 7 + [VMEM] * 2
    if needs_corners(runs):
        args += corners
        in_specs += [HBM] * 2
    if final:
        args += [hidden, *carried]
        in_specs += [ANY] + [VMEM] * len(carried)
    out_shape = [shape(C, count, COLS)] * 2 + [shape(C, LANES)] * 2 if final else [shape(ROWS, C, WIDE)] + EDGES
    scratch = [pltpu.VMEM((count, C, n), jnp.bfloat16) for n in ((WIDE, WIDE) if final else (WIDE, LANES, LANES))]
    return pl.pallas_call(
        functools.partial(conv_kernel, int(final), runs, len(carried)),
        in_specs=in_specs,
        out_specs=[VMEM if final else HBM] * len(out_shape),
        out_shape=out_shape,
        scratch_shapes=scratch
        + [pltpu.VMEM((high - low, C, n), jnp.bfloat16) for n in (WIDE, LANES, LANES, WIDE, WIDE)]
        + [pltpu.VMEM((2, CORNER, C, LANES), jnp.bfloat16)]
        + [pltpu.SemaphoreType.DMA((96,))],
        compiler_params=PARAMS,
        name="second" if final else "first",
    )(*args)


def behind_kernel(*refs):
    del refs


def behind(cells):
    return pl.pallas_call(
        behind_kernel,
        in_specs=[HBM] * len(cells),
        out_specs=[HBM] * len(cells),
        out_shape=[shape(*x.shape) for x in cells],
        input_output_aliases={i: i for i in range(len(cells))},
        compiler_params=PARAMS,
        name="behind",
    )(*cells)


def flat(weight):
    return jnp.transpose(weight, (1, 0, 2)).reshape(C, 9 * C)


def local(band_map, dilations, row_limit, weight_one, bias_one, weight_two, bias_two):
    at = whereabouts()
    vector = jnp.stack(at)
    early, late = routes(0), routes(1)

    own = [lax.ppermute(enter(i, vector, row_limit, band_map), AXES, routes(i)) for i in range(2)]
    weights = [flat(weight_one), flat(weight_two)]
    biases = [bias_one[:, None], bias_two[:, None]]
    halos, corners = exchange(at, *pack(vector, *own, weights + biases))
    hidden, *edges = conv(vector, dilations, row_limit, own, halos, corners, weights[0], biases[0])
    halos, corners = exchange(at, *edges)

    pos, off = lax.axis_index("pos"), lax.axis_index("off")
    here = lambda pairs: functools.reduce(jnp.logical_or, [(pos % 2 == s) & (off == b) for s, b in pairs])
    stays, relayed = here(STAY), here(VIA)
    leave, arrive = [], []
    for to, at_work in early:
        stored, block = to // 8, to % 8
        if (stored % 2, block) in VIA:
            via = device(stored // 2, *VIA[stored % 2, block])
            leave.append((at_work, via))
            arrive.append((via, to))
        elif at_work != to:
            leave.append((at_work, to))

    def second(rows, carried):
        return conv(
            vector, dilations, row_limit, own, halos, corners, weights[1], biases[1], hidden, rows, carried
        )

    def sorted_out(first, passed, ended):
        return jnp.where(stays, first, jnp.where(relayed, ended, passed))

    straight = [(b, a) for a, b in late]
    first, late_first, *carried = second(PARTS[0], [])
    passed = lax.ppermute(first, AXES, leave)
    direct = lax.ppermute(late_first, AXES, straight)
    more, late_more, *carried = second(PARTS[1], carried)
    passed, direct, more, late_more, edge, other = behind((passed, direct, more, late_more, *carried))
    passed_more = lax.ppermute(more, AXES, leave)
    direct_more = lax.ppermute(late_more, AXES, straight)
    ended = lax.ppermute(passed, AXES, arrive)
    ended_more = lax.ppermute(passed_more, AXES, arrive)
    gots = [sorted_out(first, passed, ended), sorted_out(more, passed_more, ended_more)]
    directs = [direct, direct_more]

    to_first = lambda core: [(place(s, f), home(s // 2, f + 1)) for s, f in CELLS if s % 2 == core]
    to_second = lambda core: [(place(s, f), home(s // 2, 8 - f)) for s, f in CELLS if s % 2 == core and f]
    edge = lax.ppermute(edge, AXES, to_first(0) + to_second(1))
    other = lax.ppermute(other, AXES, to_second(0) + to_first(1))
    low = at[STORED_BLOCK] <= 4
    halves = jnp.where(low, edge, other), jnp.where(low, other, edge)
    top_first = at[EARLY] == 0
    column = lax.broadcasted_iota(jnp.int32, (1, 1, COLS), 2)
    out = []
    for half in range(2):
        pieces = []
        for runs, *pair in zip(PARTS, gots, directs):
            got = jnp.where(top_first, *(pair if half == 0 else pair[::-1]))
            at_row = 0
            for start, count in runs:
                cells = lax.slice_in_dim(got, at_row, at_row + count, axis=1)
                edge = lax.slice_in_dim(halves[half], start, start + count, axis=1)[:, :, None]
                more = (cells.astype(jnp.float32) + 0.5 * edge.astype(jnp.float32)).astype(jnp.bfloat16)
                pieces.append((start, jnp.where(column == 0, more, cells)))
                at_row += count
        out += [piece for _, piece in sorted(pieces, key=lambda x: x[0])]
    return jnp.concatenate(out, axis=1)


def solution(mesh):
    in_specs = (P(None, "pos", "off"), P(), P(), P(), P(), P(), P())
    out_specs = P(None, "pos", "off")
    return jax.shard_map(local, mesh=mesh, in_specs=in_specs, out_specs=out_specs, check_vma=False)
```
